32 devices in a mesh: freq: 8 (over z, x), bl: 4 (over y, core).
Axes of the slice: x: 2, y: 2, z: 4, core: 2. Of those that a mesh axis runs over, the one named last changes fastest.
Arguments:
- vis_time: bfloat16 [8, 2, 1024, 2048], P('freq', None, 'bl'), may hold values from -6 to 6
- owner: int32 [24, 1], replicated, may hold values from 0 to 7; in each aligned block of 24 rows (0 to 23, 24 to 47, ...) at most 4 rows name the same one
- counts: int32 [24, 8], replicated, may hold values from 1 to 4
- factors: bfloat16 [32, 8, 2, 4, 1024], P('freq', None, None, None, 'bl'), may hold values from -0.1875 to 0.1875
Outputs:
- filtered: bfloat16 [8, 2, 1024, 24], P('freq', None, 'bl')
The draws below stay inside these ranges and needn't reach their ends.
Inputs may be any that keep to these rules, and one draw needn't show every extreme that they name: `owner`: every index of freq owns at least one m and at most 4; some index owns exactly 4.
All inputs are finite; a program needn't handle non-finite values.
Results may differ from the reference program's by a relative error of at most 0.0064.
Values may be sent and summed in bfloat16 or wider, within the bound.
A program may use at most 64 MiB of HBM per device.

```python
import math
import jax
import jax.numpy as jnp
import numpy as np
from jax import lax

NB = 1024
NT = 2048
K = 4
NF = 8
MM = 24
CAP = 4
SLOTS = 32
N_FREQ = 8


def touch_ends(result, stream_key, low, high):
    longest = result.shape.index(max(result.shape))
    spots = []
    for shift in (0, 1):
        where = [jax.random.randint(jax.random.fold_in(stream_key, axis), (), 0, length) for axis, length in enumerate(result.shape)]
        where[longest] = (where[longest] + shift) % result.shape[longest]
        spots.append(tuple(where))
    return result.at[spots[0]].set(low).at[spots[1]].set(high)


def level_of(stream_key, extent, pieces, low, high):
    loudness, own = 1.0, jax.random.fold_in(stream_key, 6)
    for position, parts in pieces:
        draws = jnp.exp(jax.random.uniform(jax.random.fold_in(own, position), (parts,), jnp.float32, low / len(pieces), high / len(pieces)))
        loudness = loudness * jnp.repeat(draws, extent[position] // parts).reshape([-1 if axis == position else 1 for axis in range(len(extent))])
    return loudness


def shared_out(stream_key, own, number, rows, amount, top, reach, lean):
    sequence = jax.random.permutation(stream_key, amount)
    heavy_load, common = load_shares(amount, rows * top, reach, lean, True), load_shares(amount, rows * top, reach, lean, False)
    places = jnp.arange(amount)

    def named(tallies, turn):
        used = int((tallies > 0).sum())
        fixed = max(1, used // 4)
        shifted = fixed + (places - fixed + turn * (used - fixed)) % max(1, amount - fixed)
        return jnp.zeros((amount,), jnp.int32).at[sequence[jnp.where(places < fixed, places, shifted)]].set(jnp.asarray(tallies, jnp.int32))

    tallies = jnp.where(number % 4 == 0, named(heavy_load, number // 4), named(common, number - number // 4 - 1))
    mixed = jax.random.permutation(jax.random.fold_in(own, 3), amount)
    giver, receiver = mixed[0:amount // 2 * 2:2], mixed[1:amount // 2 * 2:2]
    slack = jnp.minimum(tallies[giver] - 1, reach - tallies[receiver]) // 2
    slack = jnp.where((giver == sequence[0]) | (receiver == sequence[0]) | (tallies[receiver] == 0), 0, jnp.maximum(slack, 0))
    shifted = jax.random.randint(jax.random.fold_in(own, 4), (amount // 2,), 0, 1 << 20) % (slack + 1)
    tallies = tallies.at[giver].add(-shifted).at[receiver].add(shifted)
    members = jnp.searchsorted(jnp.cumsum(tallies), jnp.arange(rows * top), side="right").astype(jnp.int32)
    listing = members.reshape(top, rows).T
    listing = listing[jax.random.permutation(jax.random.fold_in(own, 1), rows)]
    turn = jax.random.randint(jax.random.fold_in(own, 2), (rows, 1), 0, top)
    return jnp.take_along_axis(listing, (jnp.arange(top)[None, :] + turn) % top, axis=1)


def load_shares(amount, total, bound, slope, full):
    loads = [(1 << 20) // math.isqrt(standing ** slope) + 1 for standing in range(1, amount + 1)]
    largest = bound if full else min(bound, max(-(-total // amount), total * loads[0] // sum(loads)))
    least = 1 if total - largest >= amount - 1 else 0
    holding, surplus = [largest] + [least] * (amount - 1), total - largest - least * (amount - 1)
    while surplus > 0:
        free = [i for i in range(1, amount) if holding[i] < largest] or [i for i in range(1, amount) if holding[i] < bound]
        mass, remaining = sum([loads[i] for i in free]), surplus
        for i in free:
            addition = min(bound - holding[i], max(1, remaining * loads[i] // mass), surplus)
            holding[i] = holding[i] + addition
            surplus = surplus - addition
    return np.array(holding)


def gaussian(own_key, shape, deviation, limit, shards=(), kind=jnp.bfloat16):
    drawn = deviation * jax.random.normal(own_key, shape, jnp.float32)
    if shards:
        drawn = drawn * level_of(own_key, shape, shards, -0.22, 0.18)
    return jnp.clip(drawn, -limit, limit).astype(kind)


def setup_inputs(seed: int = 0) -> dict:
    arg_keys = jax.random.split(jax.random.key(seed), 5)
    vis_time = gaussian(arg_keys[0], (NF, 2, NB, NT), 1.0, 6.0, ((0, 8), (2, 4)))
    owner_keys = jax.random.split(jax.random.fold_in(arg_keys[1], 1), MM // MM)
    owner_turns = jax.random.permutation(jax.random.fold_in(arg_keys[1], 3), MM // MM)
    owner = jax.vmap(lambda own, number: shared_out(jax.random.fold_in(arg_keys[1], 2), own, number, MM, N_FREQ, 1, CAP, 2))(owner_keys, owner_turns).reshape((MM, 1))
    counts = touch_ends(jax.random.randint(arg_keys[2], (MM, NF), 1, K + 1), jax.random.fold_in(arg_keys[2], 1), 1, K).astype(jnp.int32)
    factors = gaussian(arg_keys[3], (SLOTS, NF, 2, K, NB), NB ** -0.5, 0.1875, ((0, 8), (4, 4)))
    return {"vis_time": vis_time, "owner": owner, "counts": counts, "factors": factors}


def wave_tables(columns, samples):
    times = jnp.arange(samples, dtype=jnp.int32)
    phases = times[:, None] * columns[None, :] % samples
    angles = phases.astype(jnp.float32) * (2.0 * math.pi / samples)
    factor_scale = 1.0 / math.sqrt(samples)
    return jnp.concatenate([jnp.cos(angles) * factor_scale, jnp.sin(angles) * factor_scale], axis=1).astype(jnp.bfloat16)

def reference(vis_time, owner, counts, factors):
    owners_of = owner[:, 0]
    owner_ids = jnp.arange(N_FREQ, dtype=jnp.int32)
    onehot = (owners_of[:, None] == owner_ids[None, :]).astype(jnp.int32)
    before = jnp.cumsum(onehot, axis=0) - onehot
    ranking = lax.optimization_barrier(jnp.sum(before * onehot, axis=1))
    slot_of = (owners_of * CAP + ranking).astype(jnp.int32)
    wave_table = wave_tables(jnp.arange(MM, dtype=jnp.int32), NT)
    flattened = vis_time.reshape(NF * 2 * NB, NT)
    spectra = jnp.dot(flattened, wave_table, preferred_element_type=jnp.float32).reshape(NF, 2, NB, 2, MM)
    real_part = spectra[:, 0, :, 0] + spectra[:, 1, :, 1]
    imag_part = spectra[:, 1, :, 0] - spectra[:, 0, :, 1]
    m_modes = jnp.stack([real_part, imag_part], axis=1).astype(jnp.bfloat16)
    factor_scale = math.sqrt(NB / K)
    rank_ids = jnp.arange(K, dtype=jnp.int32)

    def one_mode(mode_index):
        slot_index = slot_of[mode_index]
        factor = lax.dynamic_index_in_dim(factors, slot_index, 0, keepdims=False).astype(jnp.float32)
        m_column = lax.dynamic_index_in_dim(m_modes, mode_index, 3, keepdims=False).astype(jnp.float32)
        fac_re, fac_im = (factor[:, 0], factor[:, 1])
        vis_re, vis_im = (m_column[:, 0], m_column[:, 1])
        coef_re = jnp.einsum('fkb,fb->fk', fac_re, vis_re) + jnp.einsum('fkb,fb->fk', fac_im, vis_im)
        coef_im = jnp.einsum('fkb,fb->fk', fac_re, vis_im) - jnp.einsum('fkb,fb->fk', fac_im, vis_re)
        limits = lax.dynamic_index_in_dim(counts, mode_index, 0, keepdims=False)
        retained = rank_ids[None, :] < limits[:, None]
        kept_re = jnp.where(retained, coef_re, 0.0).astype(jnp.bfloat16)
        kept_im = jnp.where(retained, coef_im, 0.0).astype(jnp.bfloat16)
        kept_re, kept_im = lax.optimization_barrier((kept_re, kept_im))
        kept_re = kept_re.astype(jnp.float32)
        kept_im = kept_im.astype(jnp.float32)
        syn_re = (jnp.einsum('fkb,fk->fb', fac_re, kept_re) - jnp.einsum('fkb,fk->fb', fac_im, kept_im)) * factor_scale
        syn_im = (jnp.einsum('fkb,fk->fb', fac_re, kept_im) + jnp.einsum('fkb,fk->fb', fac_im, kept_re)) * factor_scale
        return jnp.stack([syn_re, syn_im], axis=1).astype(jnp.bfloat16)
    synthesis = lax.map(one_mode, jnp.arange(MM, dtype=jnp.int32))
    return jnp.transpose(synthesis, (1, 2, 3, 0))
```

```python
import functools
import math

import jax
import jax.numpy as jnp
import numpy as np
from jax import lax
from jax.experimental import pallas as pl
from jax.experimental.pallas import tpu as pltpu
from jax.sharding import PartitionSpec as P

NB = 1024
CHUNKS = 4
F32 = jnp.float32
BF16 = jnp.bfloat16
MESH = pl.DeviceIdType.MESH


def wave_table(modes, half, samples):
    times = np.arange(samples, dtype=np.int64)[:, None]
    phases = times * np.arange(modes, dtype=np.int64)[None, :] % samples
    angles = phases * (2.0 * math.pi / samples)
    table = np.zeros((samples, 2 * half), np.float32)
    table[:, :modes] = np.cos(angles) / math.sqrt(samples)
    table[:, half : half + modes] = np.sin(angles) / math.sqrt(samples)
    return table.astype(BF16)


def flip(index, bits):
    place = 1
    while place <= bits:
        if bits & place:
            index = index + place * (1 - 2 * ((index // place) % 2))
        place *= 2
    return index


def kernel(
    dims, vis_ref, table_ref, owner_ref, counts_ref, factors_ref, out_ref,
    vis, table, held, spread, part, vis_sem, table_sem, send_sem, recv_sem, part_send, part_recv,
):
    n_freq, n_bl, modes, half, capacity, ranks = dims
    lanes = 2 * half
    rows = capacity * 2 * ranks
    group = min(n_freq, 8)
    deep = group * rows
    step = vis.shape[2]
    base_here = CHUNKS * step
    me = lax.axis_index("freq")
    mine = lax.axis_index("bl")

    def each_peer(body):
        if n_freq == 8:
            for bits in (6, 4, 7, 5, 2, 3, 1):
                other = flip(me, bits)
                body(bits, other, other)
        else:
            def turn(d, carry):
                body(d, lax.rem(me + d, n_freq), lax.rem(me + n_freq - d, n_freq))
                return carry

            lax.fori_loop(1, n_freq, turn, 0)

    barrier = pltpu.get_barrier_semaphore()

    def greet(d, to, source):
        pl.semaphore_signal(barrier, inc=1, device_id={"freq": to}, device_id_type=MESH)

    each_peer(greet)
    for d in range(1, n_bl):
        pl.semaphore_signal(
            barrier, inc=1, device_id={"bl": lax.rem(mine + d, n_bl)}, device_id_type=MESH
        )
    table_copy = pltpu.make_async_copy(table_ref, table, table_sem)
    table_copy.start()

    def vis_copy(c):
        rows_here = pl.ds(c * step, step)
        return pltpu.make_async_copy(vis_ref.at[0, :, rows_here], vis.at[:, c], vis_sem.at[c])

    for c in range(CHUNKS):
        vis_copy(c).start()
    pl.semaphore_wait(barrier, n_freq - 1 + n_bl - 1)

    def factor_copy(d, to, at):
        return pltpu.make_async_remote_copy(
            src_ref=factors_ref.at[to], dst_ref=held.at[at],
            send_sem=send_sem.at[d], recv_sem=recv_sem.at[d],
            device_id={"freq": to}, device_id_type=MESH,
        )

    each_peer(lambda d, to, source: factor_copy(d, to, me).start())
    held[me] = factors_ref[me]

    lane = lax.broadcasted_iota(jnp.int32, (modes, lanes), 1)
    mode = lax.broadcasted_iota(jnp.int32, (modes, lanes), 0)
    spreading = jnp.where(lane % half == mode, 1.0, 0.0).astype(BF16)
    owner_row = jnp.broadcast_to(owner_ref[...] + 1, (8, modes)).astype(F32).astype(BF16)
    owner_lanes = jnp.dot(owner_row, spreading, preferred_element_type=F32)[:1] - 1.0
    counts_row = jnp.broadcast_to(counts_ref[pl.ds(me, 1), :], (8, modes)).astype(F32).astype(BF16)
    counts_lanes = jnp.dot(counts_row, spreading, preferred_element_type=F32)
    owner_ids = lax.broadcasted_iota(jnp.int32, (n_freq, lanes), 0).astype(F32)
    onehot = jnp.where(owner_lanes == owner_ids, 1.0, 0.0)
    first = lax.broadcasted_iota(jnp.int32, (lanes, lanes), 0)
    second = lax.broadcasted_iota(jnp.int32, (lanes, lanes), 1)
    earlier = (first < second) & (first // half == second // half)
    earlier = jnp.where(earlier, 1.0, 0.0).astype(BF16)
    before = jnp.dot(onehot.astype(BF16), earlier, preferred_element_type=F32)
    ranking = jnp.sum(before * onehot, axis=0, keepdims=True)
    slot = owner_lanes * capacity + ranking
    slot_col = jnp.broadcast_to(slot, (8, lanes)).T[:, :1]
    scale = math.sqrt(NB / ranks)
    for g in range(n_freq // group):
        col = lax.broadcasted_iota(jnp.int32, (lanes, deep), 1) // (2 * ranks)
        col = (col + g * group * capacity).astype(F32)
        spread[g] = jnp.where(slot_col == col, scale, 0.0).astype(spread.dtype)

    table_copy.wait()
    pieces = []
    low = lax.broadcasted_iota(jnp.int32, (step, lanes), 1) < half
    for c in range(CHUNKS):
        vis_copy(c).wait()
        real = jnp.dot(vis[0, c], table[...], preferred_element_type=F32)
        imag = jnp.dot(vis[1, c], table[...], preferred_element_type=F32)
        piece = jnp.where(low, real, -real) + pltpu.roll(imag, half, 1)
        pieces.append(piece.astype(BF16))
    spectrum = jnp.concatenate(pieces, axis=0)

    each_peer(lambda d, to, source: factor_copy(d, to, source).wait_recv())
    total = jnp.zeros((2 * ranks, lanes), F32)
    for g in range(n_freq // group):
        factor = held[g * group : (g + 1) * group].reshape(deep, base_here)
        dense = jnp.dot(factor, spectrum, preferred_element_type=F32)
        row = lax.broadcasted_iota(jnp.int32, (deep, lanes), 0) // (2 * ranks)
        row = (row + g * group * capacity).astype(F32)
        chosen = jnp.where(slot == row, dense, 0.0)
        total = total + chosen.reshape(group * capacity, 2 * ranks, lanes).sum(axis=0)
    rank_row = lax.broadcasted_iota(jnp.int32, (2 * ranks, lanes), 0)
    in_low = lax.broadcasted_iota(jnp.int32, (2 * ranks, lanes), 1) < half
    crossed = pltpu.roll(pltpu.roll(total, ranks, 0), half, 1)
    part[mine] = total + jnp.where(in_low == (rank_row < ranks), crossed, -crossed)

    def part_copy(d, at):
        return pltpu.make_async_remote_copy(
            src_ref=part.at[mine], dst_ref=part.at[at],
            send_sem=part_send.at[d], recv_sem=part_recv.at[d],
            device_id={"bl": lax.rem(mine + d, n_bl)}, device_id_type=MESH,
        )

    for d in range(1, n_bl):
        part_copy(d, mine).start()
    for d in range(1, n_bl):
        part_copy(d, lax.rem(mine + n_bl - d, n_bl)).wait_recv()
    summed = part[0]
    for b in range(1, n_bl):
        summed = summed + part[b]
    kept = jnp.where((rank_row % ranks).astype(F32) < counts_lanes, summed, 0.0).astype(BF16)

    tiling = lax.broadcasted_iota(jnp.int32, (2 * ranks, deep), 1) % (2 * ranks)
    tiling = jnp.where(
        tiling == lax.broadcasted_iota(jnp.int32, (2 * ranks, deep), 0), 1.0, 0.0
    ).astype(BF16)
    tiled = lax.dot_general(
        kept, tiling, (((0,), (0,)), ((), ())), preferred_element_type=F32
    )
    filtered = jnp.zeros((lanes, base_here), F32)
    for g in range(n_freq // group):
        factor = held[g * group : (g + 1) * group].reshape(deep, base_here)
        weight = (tiled * spread[g].astype(F32)).astype(BF16)
        filtered = filtered + jnp.dot(weight, factor, preferred_element_type=F32)
    filtered = filtered.astype(BF16)
    out_ref[0] = filtered[:modes]
    out_ref[1] = filtered[half : half + modes]
    each_peer(lambda d, to, source: factor_copy(d, to, me).wait_send())
    for d in range(1, n_bl):
        part_copy(d, mine).wait_send()


def local(n_freq, n_bl, vis_time, owner, counts, factors):
    _, _, base_here, samples = vis_time.shape
    modes = owner.shape[0]
    capacity, _, _, ranks, _ = factors.shape
    half = -(-2 * modes // 128) * 64
    rows = capacity * 2 * ranks
    group = min(n_freq, 8)
    table = jnp.asarray(wave_table(modes, half, samples))
    moved = factors.transpose(1, 0, 2, 3, 4).reshape(n_freq, rows, base_here)
    vmem = pl.BlockSpec(memory_space=pltpu.VMEM)
    anywhere = pl.BlockSpec(memory_space=pl.ANY)
    out = pl.pallas_call(
        functools.partial(kernel, (n_freq, n_bl, modes, half, capacity, ranks)),
        out_shape=jax.ShapeDtypeStruct((2, modes, base_here), BF16),
        in_specs=[anywhere, anywhere, vmem, vmem, vmem],
        out_specs=vmem,
        scratch_shapes=[
            pltpu.VMEM((2, CHUNKS, base_here // CHUNKS, samples), BF16),
            pltpu.VMEM((samples, 2 * half), BF16),
            pltpu.VMEM((n_freq, rows, base_here), BF16),
            pltpu.VMEM((n_freq // group, 2 * half, group * rows), BF16),
            pltpu.VMEM((n_bl, 2 * ranks, 2 * half), F32),
            pltpu.SemaphoreType.DMA((CHUNKS,)),
            pltpu.SemaphoreType.DMA,
            pltpu.SemaphoreType.DMA((n_freq,)),
            pltpu.SemaphoreType.DMA((n_freq,)),
            pltpu.SemaphoreType.DMA((n_bl,)),
            pltpu.SemaphoreType.DMA((n_bl,)),
        ],
        compiler_params=pltpu.CompilerParams(
            collective_id=0, has_side_effects=True, vmem_limit_bytes=48 * 1024 * 1024
        ),
    )(vis_time, table, owner.T, counts.T, moved)
    return out.transpose(0, 2, 1)[None]


def solution(mesh):
    placed = (P("freq", None, "bl", None), P(), P(), P("freq", None, None, None, "bl"))
    return jax.shard_map(
        functools.partial(local, mesh.shape["freq"], mesh.shape["bl"]),
        mesh=mesh, in_specs=placed, out_specs=P("freq", None, "bl", None), check_vma=False,
    )
```

```python
import functools
import math

import jax
import jax.numpy as jnp
import numpy as np
from jax import lax
from jax.experimental import pallas as pl
from jax.experimental.pallas import tpu as pltpu
from jax.sharding import PartitionSpec as P

NB = 1024
CHUNKS = 4
F32 = jnp.float32
BF16 = jnp.bfloat16
MESH = pl.DeviceIdType.MESH


def wave_table(modes, half, samples):
    times = np.arange(samples, dtype=np.int64)[:, None]
    phases = times * np.arange(modes, dtype=np.int64)[None, :] % samples
    angles = phases * (2.0 * math.pi / samples)
    table = np.zeros((samples, 2 * half), np.float32)
    table[:, :modes] = np.cos(angles) / math.sqrt(samples)
    table[:, half : half + modes] = np.sin(angles) / math.sqrt(samples)
    return table.astype(BF16)


def flip(index, bits):
    place = 1
    while place <= bits:
        if bits & place:
            index = index + place * (1 - 2 * ((index // place) % 2))
        place *= 2
    return index


def kernel(
    dims, vis_ref, table_ref, owner_ref, counts_ref, factors_ref, out_ref,
    vis, table, owner, counts, held, packed, spread, part,
    vis_sem, table_sem, small_sem, send_sem, recv_sem, part_send, part_recv,
):
    n_freq, n_bl, modes, half, capacity, ranks = dims
    lanes = 2 * half
    rows = capacity * 2 * ranks
    group = min(n_freq // 2, 4)
    deep = group * rows
    blocks = n_freq // group
    base_here, step = vis.shape[2], vis.shape[3]
    me = lax.axis_index("freq")
    mine = lax.axis_index("bl")

    def peers(body, chosen=None):
        if n_freq == 8:
            for bits in chosen or (6, 4, 7, 5, 2, 3, 1):
                other = flip(me, bits)
                body(bits, other, other)
        elif chosen is None or chosen[0] == 1:
            def turn(d, carry):
                body(d, lax.rem(me + d, n_freq), lax.rem(me + n_freq - d, n_freq))
                return carry

            lax.fori_loop(1, n_freq, turn, 0)

    barrier = pltpu.get_barrier_semaphore()

    def greet(d, to, source):
        pl.semaphore_signal(barrier, inc=1, device_id={"freq": to}, device_id_type=MESH)

    peers(greet)
    for d in range(1, n_bl):
        pl.semaphore_signal(
            barrier, inc=1, device_id={"bl": lax.rem(mine + d, n_bl)}, device_id_type=MESH
        )

    def vis_copy(c):
        return pltpu.make_async_copy(
            vis_ref.at[0, :, :, pl.ds(c * step, step)], vis.at[c], vis_sem.at[c]
        )

    def table_copy(c):
        times = pl.ds(c * step, step)
        return pltpu.make_async_copy(table_ref.at[times], table.at[times], table_sem.at[c])

    owner_copy = pltpu.make_async_copy(owner_ref, owner, small_sem.at[0])
    counts_copy = pltpu.make_async_copy(counts_ref, counts, small_sem.at[1])
    own_copy = pltpu.make_async_copy(factors_ref.at[:, me], held.at[me], small_sem.at[2])
    owner_copy.start()
    counts_copy.start()
    for c in range(CHUNKS):
        table_copy(c).start()
        vis_copy(c).start()
    own_copy.start()
    pl.semaphore_wait(barrier, n_freq - 1 + n_bl - 1)

    def factor_copy(d, to, at):
        return pltpu.make_async_remote_copy(
            src_ref=factors_ref.at[:, to], dst_ref=held.at[at],
            send_sem=send_sem.at[d], recv_sem=recv_sem.at[d],
            device_id={"freq": to}, device_id_type=MESH,
        )

    peers(lambda d, to, source: factor_copy(d, to, me).start())

    owner_copy.wait()
    counts_copy.wait()
    lane = lax.broadcasted_iota(jnp.int32, (modes, lanes), 1)
    mode = lax.broadcasted_iota(jnp.int32, (modes, lanes), 0)
    spreading = jnp.where(lane % half == mode, 1.0, 0.0).astype(BF16)
    owner_row = jnp.broadcast_to(owner[...] + 1, (8, modes)).astype(F32).astype(BF16)
    owner_lanes = jnp.dot(owner_row, spreading, preferred_element_type=F32)[:1] - 1.0
    counts_row = jnp.broadcast_to(counts[pl.ds(me, 1), :], (8, modes)).astype(F32).astype(BF16)
    counts_lanes = jnp.dot(counts_row, spreading, preferred_element_type=F32)
    owner_ids = lax.broadcasted_iota(jnp.int32, (n_freq, lanes), 0).astype(F32)
    onehot = jnp.where(owner_lanes == owner_ids, 1.0, 0.0)
    first = lax.broadcasted_iota(jnp.int32, (lanes, lanes), 0)
    second = lax.broadcasted_iota(jnp.int32, (lanes, lanes), 1)
    earlier = (first < second) & (first // half == second // half)
    earlier = jnp.where(earlier, 1.0, 0.0).astype(BF16)
    before = jnp.dot(onehot.astype(BF16), earlier, preferred_element_type=F32)
    ranking = jnp.sum(before * onehot, axis=0, keepdims=True)
    slot = owner_lanes * capacity + ranking
    slot_col = jnp.broadcast_to(slot, (8, lanes)).T[:, :1]
    scale = math.sqrt(NB / ranks)
    for g in range(blocks):
        col = lax.broadcasted_iota(jnp.int32, (lanes, deep), 1) // (2 * ranks)
        col = (col + g * group * capacity).astype(F32)
        spread[g] = jnp.where(slot_col == col, scale, 0.0).astype(spread.dtype)

    spectra = jnp.zeros((2 * base_here, lanes), F32)
    for c in range(CHUNKS):
        table_copy(c).wait()
        vis_copy(c).wait()
        spectra = spectra + jnp.dot(
            vis[c].reshape(2 * base_here, step), table[c * step : (c + 1) * step],
            preferred_element_type=F32,
        )
    real, imag = spectra[:base_here], spectra[base_here:]
    low = lax.broadcasted_iota(jnp.int32, (base_here, lanes), 1) < half
    spectrum = (jnp.where(low, real, -real) + pltpu.roll(imag, half, 1)).astype(BF16)

    def coefficients(block):
        from_here = pl.ds(block * group, group)
        factor = held[from_here].reshape(deep, base_here)
        packed[block] = factor
        dense = jnp.dot(factor, spectrum, preferred_element_type=F32)
        row = lax.broadcasted_iota(jnp.int32, (deep, lanes), 0) // (2 * ranks)
        row = (row + block * group * capacity).astype(F32)
        chosen = jnp.where(slot == row, dense, 0.0)
        return chosen.reshape(group * capacity, 2 * ranks, lanes).sum(axis=0)

    own_copy.wait()
    total = jnp.zeros((2 * ranks, lanes), F32)
    peers(lambda d, to, source: factor_copy(d, to, source).wait_recv(), (1, 2, 3))
    for b in range(blocks):
        if b == 1:
            peers(lambda d, to, source: factor_copy(d, to, source).wait_recv(), (4, 5, 6, 7))
        total = total + coefficients(lax.rem(me // group + b, blocks))
    rank_row = lax.broadcasted_iota(jnp.int32, (2 * ranks, lanes), 0)
    in_low = lax.broadcasted_iota(jnp.int32, (2 * ranks, lanes), 1) < half
    crossed = pltpu.roll(pltpu.roll(total, ranks, 0), half, 1)
    part[mine] = total + jnp.where(in_low == (rank_row < ranks), crossed, -crossed)

    def part_copy(d, at):
        return pltpu.make_async_remote_copy(
            src_ref=part.at[mine], dst_ref=part.at[at],
            send_sem=part_send.at[d], recv_sem=part_recv.at[d],
            device_id={"bl": lax.rem(mine + d, n_bl)}, device_id_type=MESH,
        )

    for d in range(1, n_bl):
        part_copy(d, mine).start()
    for d in range(1, n_bl):
        part_copy(d, lax.rem(mine + n_bl - d, n_bl)).wait_recv()
    summed = part[0]
    for b in range(1, n_bl):
        summed = summed + part[b]
    kept = jnp.where((rank_row % ranks).astype(F32) < counts_lanes, summed, 0.0).astype(BF16)

    tiling = lax.broadcasted_iota(jnp.int32, (2 * ranks, deep), 1) % (2 * ranks)
    tiling = jnp.where(
        tiling == lax.broadcasted_iota(jnp.int32, (2 * ranks, deep), 0), 1.0, 0.0
    ).astype(BF16)
    tiled = lax.dot_general(
        kept, tiling, (((0,), (0,)), ((), ())), preferred_element_type=F32
    )
    filtered = jnp.zeros((lanes, base_here), F32)
    for g in range(blocks):
        weight = (tiled * spread[g].astype(F32)).astype(BF16)
        filtered = filtered + jnp.dot(weight, packed[g], preferred_element_type=F32)
    filtered = filtered.astype(BF16)
    out_ref[0] = filtered[:modes]
    out_ref[1] = filtered[half : half + modes]
    peers(lambda d, to, source: factor_copy(d, to, me).wait_send())
    for d in range(1, n_bl):
        part_copy(d, mine).wait_send()


def local(n_freq, n_bl, vis_time, owner, counts, factors):
    _, _, base_here, samples = vis_time.shape
    modes = owner.shape[0]
    capacity, _, _, ranks, _ = factors.shape
    half = -(-2 * modes // 128) * 64
    rows = capacity * 2 * ranks
    group = min(n_freq // 2, 4)
    table = jnp.asarray(wave_table(modes, half, samples))
    stays = pl.BlockSpec(memory_space=pltpu.HBM)
    out = pl.pallas_call(
        functools.partial(kernel, (n_freq, n_bl, modes, half, capacity, ranks)),
        out_shape=jax.ShapeDtypeStruct((2, modes, base_here), BF16),
        in_specs=[stays] * 5,
        out_specs=pl.BlockSpec(memory_space=pltpu.VMEM),
        scratch_shapes=[
            pltpu.VMEM((CHUNKS, 2, base_here, samples // CHUNKS), BF16),
            pltpu.VMEM((samples, 2 * half), BF16),
            pltpu.VMEM((1, modes), jnp.int32),
            pltpu.VMEM((n_freq, modes), jnp.int32),
            pltpu.VMEM((n_freq, capacity, 2, ranks, base_here), BF16),
            pltpu.VMEM((n_freq // group, group * rows, base_here), BF16),
            pltpu.VMEM((n_freq // group, 2 * half, group * rows), BF16),
            pltpu.VMEM((n_bl, 2 * ranks, 2 * half), F32),
            pltpu.SemaphoreType.DMA((CHUNKS,)),
            pltpu.SemaphoreType.DMA((CHUNKS,)),
            pltpu.SemaphoreType.DMA((3,)),
            pltpu.SemaphoreType.DMA((n_freq,)),
            pltpu.SemaphoreType.DMA((n_freq,)),
            pltpu.SemaphoreType.DMA((n_bl,)),
            pltpu.SemaphoreType.DMA((n_bl,)),
        ],
        compiler_params=pltpu.CompilerParams(
            collective_id=0, has_side_effects=True, vmem_limit_bytes=63 * 1024 * 1024
        ),
    )(vis_time, table, owner.T, counts.T, factors)
    return out.transpose(0, 2, 1)[None]


def solution(mesh):
    placed = (P("freq", None, "bl", None), P(), P(), P("freq", None, None, None, "bl"))
    return jax.shard_map(
        functools.partial(local, mesh.shape["freq"], mesh.shape["bl"]),
        mesh=mesh, in_specs=placed, out_specs=P("freq", None, "bl", None), check_vma=False,
    )
```

```python
import functools
import math

import jax
import jax.numpy as jnp
import numpy as np
from jax import lax
from jax.experimental import pallas as pl
from jax.experimental.pallas import tpu as pltpu
from jax.sharding import PartitionSpec as P

NB = 1024
CHUNKS = 4
F32 = jnp.float32
BF16 = jnp.bfloat16
MESH = pl.DeviceIdType.MESH


def wave_table(modes, half, samples):
    times = np.arange(samples, dtype=np.int64)[:, None]
    phases = times * np.arange(modes, dtype=np.int64)[None, :] % samples
    angles = phases * (2.0 * math.pi / samples)
    table = np.zeros((samples, 2 * half), np.float32)
    table[:, :modes] = np.cos(angles) / math.sqrt(samples)
    table[:, half : half + modes] = np.sin(angles) / math.sqrt(samples)
    return table.astype(BF16)


def flip(index, bits):
    place = 1
    while place <= bits:
        if bits & place:
            index = index + place * (1 - 2 * ((index // place) % 2))
        place *= 2
    return index


def kernel(
    dims, vis_ref, table_ref, owner_ref, counts_ref, factors_ref, out_ref,
    vis, table, owner, counts, held, packed, spread, part,
    vis_sem, table_sem, small_sem, send_sem, recv_sem, part_send, part_recv,
):
    n_freq, n_bl, modes, half, capacity, ranks = dims
    lanes = 2 * half
    rows = capacity * 2 * ranks
    group = min(n_freq // 2, 4)
    deep = group * rows
    blocks = n_freq // group
    base_here, step = vis.shape[2], vis.shape[3]
    me = lax.axis_index("freq")
    mine = lax.axis_index("bl")

    def peers(body, chosen=None):
        if n_freq == 8:
            for bits in chosen or (6, 4, 7, 5, 2, 3, 1):
                other = flip(me, bits)
                body(bits, other, other)
        elif chosen is None or chosen[0] == 1:
            def turn(d, carry):
                body(d, lax.rem(me + d, n_freq), lax.rem(me + n_freq - d, n_freq))
                return carry

            lax.fori_loop(1, n_freq, turn, 0)

    barrier = pltpu.get_barrier_semaphore()

    def greet(d, to, source):
        pl.semaphore_signal(barrier, inc=1, device_id={"freq": to}, device_id_type=MESH)

    peers(greet)
    for d in range(1, n_bl):
        pl.semaphore_signal(
            barrier, inc=1, device_id={"bl": lax.rem(mine + d, n_bl)}, device_id_type=MESH
        )

    def vis_copy(c):
        return pltpu.make_async_copy(
            vis_ref.at[0, :, :, pl.ds(c * step, step)], vis.at[c], vis_sem.at[c]
        )

    def table_copy(c):
        times = pl.ds(c * step, step)
        return pltpu.make_async_copy(table_ref.at[times], table.at[times], table_sem.at[c])

    owner_copy = pltpu.make_async_copy(owner_ref, owner, small_sem.at[0])
    counts_copy = pltpu.make_async_copy(counts_ref, counts, small_sem.at[1])
    own_copy = pltpu.make_async_copy(factors_ref.at[:, me], held.at[me], small_sem.at[2])
    owner_copy.start()
    counts_copy.start()
    for c in range(CHUNKS):
        table_copy(c).start()
        vis_copy(c).start()
    own_copy.start()
    pl.semaphore_wait(barrier, n_freq - 1 + n_bl - 1)

    def factor_copy(d, to, at):
        return pltpu.make_async_remote_copy(
            src_ref=factors_ref.at[:, to], dst_ref=held.at[at],
            send_sem=send_sem.at[d], recv_sem=recv_sem.at[d],
            device_id={"freq": to}, device_id_type=MESH,
        )

    peers(lambda d, to, source: factor_copy(d, to, me).start())

    owner_copy.wait()
    counts_copy.wait()
    lane = lax.broadcasted_iota(jnp.int32, (modes, lanes), 1)
    mode = lax.broadcasted_iota(jnp.int32, (modes, lanes), 0)
    spreading = jnp.where(lane % half == mode, 1.0, 0.0).astype(BF16)
    owner_row = jnp.broadcast_to(owner[...] + 1, (8, modes)).astype(F32).astype(BF16)
    owner_lanes = jnp.dot(owner_row, spreading, preferred_element_type=F32)[:1] - 1.0
    counts_row = jnp.broadcast_to(counts[pl.ds(me, 1), :], (8, modes)).astype(F32).astype(BF16)
    counts_lanes = jnp.dot(counts_row, spreading, preferred_element_type=F32)
    owner_ids = lax.broadcasted_iota(jnp.int32, (n_freq, lanes), 0).astype(F32)
    onehot = jnp.where(owner_lanes == owner_ids, 1.0, 0.0)
    first = lax.broadcasted_iota(jnp.int32, (lanes, lanes), 0)
    second = lax.broadcasted_iota(jnp.int32, (lanes, lanes), 1)
    earlier = (first < second) & (first // half == second // half)
    earlier = jnp.where(earlier, 1.0, 0.0).astype(BF16)
    before = jnp.dot(onehot.astype(BF16), earlier, preferred_element_type=F32)
    ranking = jnp.sum(before * onehot, axis=0, keepdims=True)
    slot = owner_lanes * capacity + ranking
    slot_col = jnp.broadcast_to(slot, (8, lanes)).T[:, :1]
    scale = math.sqrt(NB / ranks)
    for g in range(blocks):
        col = lax.broadcasted_iota(jnp.int32, (lanes, deep), 1) // (2 * ranks)
        col = (col + g * group * capacity).astype(F32)
        spread[g] = jnp.where(slot_col == col, scale, 0.0).astype(spread.dtype)

    spectra = jnp.zeros((2 * base_here, lanes), F32)
    for c in range(CHUNKS):
        table_copy(c).wait()
        vis_copy(c).wait()
        spectra = spectra + jnp.dot(
            vis[c].reshape(2 * base_here, step), table[c * step : (c + 1) * step],
            preferred_element_type=F32,
        )
    real, imag = spectra[:base_here], spectra[base_here:]
    low = lax.broadcasted_iota(jnp.int32, (base_here, lanes), 1) < half
    spectrum = (jnp.where(low, real, -real) + pltpu.roll(imag, half, 1)).astype(BF16)

    def coefficients(block):
        from_here = pl.ds(block * group, group)
        factor = held[from_here].reshape(deep, base_here)
        packed[block] = factor
        dense = jnp.dot(factor, spectrum, preferred_element_type=F32)
        row = lax.broadcasted_iota(jnp.int32, (deep, lanes), 0) // (2 * ranks)
        row = (row + block * group * capacity).astype(F32)
        chosen = jnp.where(slot == row, dense, 0.0)
        return chosen.reshape(group * capacity, 2 * ranks, lanes).sum(axis=0)

    own_copy.wait()
    total = jnp.zeros((2 * ranks, lanes), F32)
    peers(lambda d, to, source: factor_copy(d, to, source).wait_recv(), (1, 2, 3))
    for b in range(blocks):
        if b == 1:
            peers(lambda d, to, source: factor_copy(d, to, source).wait_recv(), (4, 5, 6, 7))
        total = total + coefficients(lax.rem(me // group + b, blocks))
    rank_row = lax.broadcasted_iota(jnp.int32, (2 * ranks, lanes), 0)
    in_low = lax.broadcasted_iota(jnp.int32, (2 * ranks, lanes), 1) < half
    crossed = pltpu.roll(pltpu.roll(total, ranks, 0), half, 1)
    part[mine] = total + jnp.where(in_low == (rank_row < ranks), crossed, -crossed)

    def part_copy(d, at):
        return pltpu.make_async_remote_copy(
            src_ref=part.at[mine], dst_ref=part.at[at],
            send_sem=part_send.at[d], recv_sem=part_recv.at[d],
            device_id={"bl": lax.rem(mine + d, n_bl)}, device_id_type=MESH,
        )

    for d in range(1, n_bl):
        part_copy(d, mine).start()
    for d in range(1, n_bl):
        part_copy(d, lax.rem(mine + n_bl - d, n_bl)).wait_recv()
    summed = part[0]
    for b in range(1, n_bl):
        summed = summed + part[b]
    kept = jnp.where((rank_row % ranks).astype(F32) < counts_lanes, summed, 0.0).astype(BF16)

    tiling = lax.broadcasted_iota(jnp.int32, (2 * ranks, deep), 1) % (2 * ranks)
    tiling = jnp.where(
        tiling == lax.broadcasted_iota(jnp.int32, (2 * ranks, deep), 0), 1.0, 0.0
    ).astype(BF16)
    tiled = lax.dot_general(
        kept, tiling, (((0,), (0,)), ((), ())), preferred_element_type=F32
    )
    filtered = jnp.zeros((lanes, base_here), F32)
    for g in range(blocks):
        weight = (tiled * spread[g].astype(F32)).astype(BF16)
        filtered = filtered + jnp.dot(weight, packed[g], preferred_element_type=F32)
    filtered = filtered.astype(BF16)
    out_ref[0] = filtered[:modes]
    out_ref[1] = filtered[half : half + modes]
    peers(lambda d, to, source: factor_copy(d, to, me).wait_send())
    for d in range(1, n_bl):
        part_copy(d, mine).wait_send()


def local(n_freq, n_bl, vis_time, owner, counts, factors):
    _, _, base_here, samples = vis_time.shape
    modes = owner.shape[0]
    capacity, _, _, ranks, _ = factors.shape
    half = -(-2 * modes // 128) * 64
    rows = capacity * 2 * ranks
    group = min(n_freq // 2, 4)
    table = jnp.asarray(wave_table(modes, half, samples))
    stays = pl.BlockSpec(memory_space=pltpu.HBM)
    out = pl.pallas_call(
        functools.partial(kernel, (n_freq, n_bl, modes, half, capacity, ranks)),
        out_shape=pltpu.VMEM((2, modes, base_here), BF16),
        in_specs=[stays] * 5,
        out_specs=pl.BlockSpec(memory_space=pltpu.VMEM),
        scratch_shapes=[
            pltpu.VMEM((CHUNKS, 2, base_here, samples // CHUNKS), BF16),
            pltpu.VMEM((samples, 2 * half), BF16),
            pltpu.VMEM((1, modes), jnp.int32),
            pltpu.VMEM((n_freq, modes), jnp.int32),
            pltpu.VMEM((n_freq, capacity, 2, ranks, base_here), BF16),
            pltpu.VMEM((n_freq // group, group * rows, base_here), BF16),
            pltpu.VMEM((n_freq // group, 2 * half, group * rows), BF16),
            pltpu.VMEM((n_bl, 2 * ranks, 2 * half), F32),
            pltpu.SemaphoreType.DMA((CHUNKS,)),
            pltpu.SemaphoreType.DMA((CHUNKS,)),
            pltpu.SemaphoreType.DMA((3,)),
            pltpu.SemaphoreType.DMA((n_freq,)),
            pltpu.SemaphoreType.DMA((n_freq,)),
            pltpu.SemaphoreType.DMA((n_bl,)),
            pltpu.SemaphoreType.DMA((n_bl,)),
        ],
        compiler_params=pltpu.CompilerParams(
            collective_id=0, has_side_effects=True, vmem_limit_bytes=63 * 1024 * 1024
        ),
    )(vis_time, table, owner.T, counts.T, factors)
    return out.transpose(0, 2, 1)[None]


def solution(mesh):
    placed = (P("freq", None, "bl", None), P(), P(), P("freq", None, None, None, "bl"))
    return jax.shard_map(
        functools.partial(local, mesh.shape["freq"], mesh.shape["bl"]),
        mesh=mesh, in_specs=placed, out_specs=P("freq", None, "bl", None), check_vma=False,
    )
```

```python
import functools
import math

import jax
import jax.numpy as jnp
import numpy as np
from jax import lax
from jax.experimental import pallas as pl
from jax.experimental.pallas import tpu as pltpu
from jax.sharding import PartitionSpec as P

NB = 1024
CHUNKS = 2
F32 = jnp.float32
BF16 = jnp.bfloat16
MESH = pl.DeviceIdType.MESH


def wave_table(modes, half, samples):
    times = np.arange(samples, dtype=np.int64)[:, None]
    phases = times * np.arange(modes, dtype=np.int64)[None, :] % samples
    angles = phases * (2.0 * math.pi / samples)
    table = np.zeros((samples, 2 * half), np.float32)
    table[:, :modes] = np.cos(angles) / math.sqrt(samples)
    table[:, half : half + modes] = np.sin(angles) / math.sqrt(samples)
    return table.astype(BF16)


def flip(index, bits):
    place = 1
    while place <= bits:
        if bits & place:
            index = index + place * (1 - 2 * ((index // place) % 2))
        place *= 2
    return index


def kernel(
    dims, vis_ref, table_ref, owner_ref, counts_ref, factors_ref, out_ref,
    vis, table, owner, counts, held, packed, spread, slots, limits, spectrum, part,
    vis_sem, table_sem, small_sem, send_sem, recv_sem, part_send, part_recv,
):
    n_freq, n_bl, modes, half, capacity, ranks = dims
    lanes = 2 * half
    rows = capacity * 2 * ranks
    group = min(n_freq // 2, 4)
    deep = group * rows
    blocks = n_freq // group
    base_here, step = vis.shape[2], vis.shape[3]
    me = lax.axis_index("freq")
    mine = lax.axis_index("bl")

    def peers(body, chosen=None):
        if n_freq == 8:
            for bits in chosen or (6, 4, 7, 5, 2, 3, 1):
                other = flip(me, bits)
                body(bits, other, other)
        elif chosen is None or chosen[0] == 1:
            def turn(d, carry):
                body(d, lax.rem(me + d, n_freq), lax.rem(me + n_freq - d, n_freq))
                return carry

            lax.fori_loop(1, n_freq, turn, 0)

    barrier = pltpu.get_barrier_semaphore()

    def greet(d, to, source):
        pl.semaphore_signal(barrier, inc=1, device_id={"freq": to}, device_id_type=MESH)

    peers(greet)
    for d in range(1, n_bl):
        pl.semaphore_signal(
            barrier, inc=1, device_id={"bl": lax.rem(mine + d, n_bl)}, device_id_type=MESH
        )

    def vis_copy(c):
        return pltpu.make_async_copy(
            vis_ref.at[0, :, :, pl.ds(c * step, step)], vis.at[c], vis_sem.at[c]
        )

    def table_copy(c):
        times = pl.ds(c * step, step)
        return pltpu.make_async_copy(table_ref.at[times], table.at[times], table_sem.at[c])

    owner_copy = pltpu.make_async_copy(owner_ref, owner, small_sem.at[0])
    counts_copy = pltpu.make_async_copy(counts_ref, counts, small_sem.at[1])
    own_copy = pltpu.make_async_copy(factors_ref.at[:, me], held.at[me], small_sem.at[2])

    def fetch():
        for c in range(CHUNKS):
            table_copy(c).start()
            vis_copy(c).start()
        owner_copy.start()
        counts_copy.start()
        own_copy.start()

    def factor_copy(d, to, at):
        return pltpu.make_async_remote_copy(
            src_ref=factors_ref.at[:, to], dst_ref=held.at[at],
            send_sem=send_sem.at[d], recv_sem=recv_sem.at[d],
            device_id={"freq": to}, device_id_type=MESH,
        )

    def prepare():
        owner_copy.wait()
        counts_copy.wait()
        lane = lax.broadcasted_iota(jnp.int32, (modes, lanes), 1)
        mode = lax.broadcasted_iota(jnp.int32, (modes, lanes), 0)
        spreading = jnp.where(lane % half == mode, 1.0, 0.0).astype(BF16)
        owner_row = jnp.broadcast_to(owner[...] + 1, (8, modes)).astype(F32).astype(BF16)
        owner_lanes = jnp.dot(owner_row, spreading, preferred_element_type=F32)[:1] - 1.0
        counts_row = jnp.broadcast_to(counts[pl.ds(me, 1), :], (8, modes)).astype(F32).astype(BF16)
        limits[...] = jnp.dot(counts_row, spreading, preferred_element_type=F32)
        owner_ids = lax.broadcasted_iota(jnp.int32, (n_freq, lanes), 0).astype(F32)
        onehot = jnp.where(owner_lanes == owner_ids, 1.0, 0.0)
        first = lax.broadcasted_iota(jnp.int32, (lanes, lanes), 0)
        second = lax.broadcasted_iota(jnp.int32, (lanes, lanes), 1)
        earlier = (first < second) & (first // half == second // half)
        earlier = jnp.where(earlier, 1.0, 0.0).astype(BF16)
        before = jnp.dot(onehot.astype(BF16), earlier, preferred_element_type=F32)
        ranking = jnp.sum(before * onehot, axis=0, keepdims=True)
        slot = owner_lanes * capacity + ranking
        slots[...] = jnp.broadcast_to(slot, (8, lanes))
        slot_col = jnp.broadcast_to(slot, (8, lanes)).T[:, :1]
        scale = math.sqrt(NB / ranks)
        for g in range(blocks):
            col = lax.broadcasted_iota(jnp.int32, (lanes, deep), 1) // (2 * ranks)
            col = (col + g * group * capacity).astype(F32)
            spread[g] = jnp.where(slot_col == col, scale, 0.0).astype(spread.dtype)

        spectra = jnp.zeros((2 * base_here, lanes), F32)
        for c in range(CHUNKS):
            table_copy(c).wait()
            vis_copy(c).wait()
            spectra = spectra + jnp.dot(
                vis[c].reshape(2 * base_here, step), table[c * step : (c + 1) * step],
                preferred_element_type=F32,
            )
        real, imag = spectra[:base_here], spectra[base_here:]
        low = lax.broadcasted_iota(jnp.int32, (base_here, lanes), 1) < half
        spectrum[...] = (jnp.where(low, real, -real) + pltpu.roll(imag, half, 1)).astype(BF16)

    leading = me < n_freq // 2

    @pl.when(leading)
    def _():
        fetch()
        prepare()

    pl.semaphore_wait(barrier, n_freq - 1 + n_bl - 1)
    peers(lambda d, to, source: factor_copy(d, to, me).start())

    @pl.when(jnp.logical_not(leading))
    def _():
        fetch()
        prepare()

    slot = slots[:1]
    def coefficients(block):
        from_here = pl.ds(block * group, group)
        factor = held[from_here].reshape(deep, base_here)
        packed[block] = factor
        dense = jnp.dot(factor, spectrum[...], preferred_element_type=F32)
        row = lax.broadcasted_iota(jnp.int32, (deep, lanes), 0) // (2 * ranks)
        row = (row + block * group * capacity).astype(F32)
        chosen = jnp.where(slot == row, dense, 0.0)
        return chosen.reshape(group * capacity, 2 * ranks, lanes).sum(axis=0)

    own_copy.wait()
    total = jnp.zeros((2 * ranks, lanes), F32)
    peers(lambda d, to, source: factor_copy(d, to, source).wait_recv(), (1, 2, 3))
    for b in range(blocks):
        if b == 1:
            peers(lambda d, to, source: factor_copy(d, to, source).wait_recv(), (4, 5, 6, 7))
        total = total + coefficients(lax.rem(me // group + b, blocks))
    rank_row = lax.broadcasted_iota(jnp.int32, (2 * ranks, lanes), 0)
    in_low = lax.broadcasted_iota(jnp.int32, (2 * ranks, lanes), 1) < half
    crossed = pltpu.roll(pltpu.roll(total, ranks, 0), half, 1)
    part[mine] = total + jnp.where(in_low == (rank_row < ranks), crossed, -crossed)

    def part_copy(d, at):
        return pltpu.make_async_remote_copy(
            src_ref=part.at[mine], dst_ref=part.at[at],
            send_sem=part_send.at[d], recv_sem=part_recv.at[d],
            device_id={"bl": lax.rem(mine + d, n_bl)}, device_id_type=MESH,
        )

    for d in range(1, n_bl):
        part_copy(d, mine).start()
    for d in range(1, n_bl):
        part_copy(d, lax.rem(mine + n_bl - d, n_bl)).wait_recv()
    summed = part[0]
    for b in range(1, n_bl):
        summed = summed + part[b]
    kept = jnp.where((rank_row % ranks).astype(F32) < limits[:2 * ranks], summed, 0.0).astype(BF16)

    tiling = lax.broadcasted_iota(jnp.int32, (2 * ranks, deep), 1) % (2 * ranks)
    tiling = jnp.where(
        tiling == lax.broadcasted_iota(jnp.int32, (2 * ranks, deep), 0), 1.0, 0.0
    ).astype(BF16)
    tiled = lax.dot_general(
        kept, tiling, (((0,), (0,)), ((), ())), preferred_element_type=F32
    )
    filtered = jnp.zeros((lanes, base_here), F32)
    for g in range(blocks):
        weight = (tiled * spread[g].astype(F32)).astype(BF16)
        filtered = filtered + jnp.dot(weight, packed[g], preferred_element_type=F32)
    filtered = filtered.astype(BF16)
    out_ref[0] = filtered[:modes]
    out_ref[1] = filtered[half : half + modes]
    peers(lambda d, to, source: factor_copy(d, to, me).wait_send())
    for d in range(1, n_bl):
        part_copy(d, mine).wait_send()


def local(n_freq, n_bl, vis_time, owner, counts, factors):
    _, _, base_here, samples = vis_time.shape
    modes = owner.shape[0]
    capacity, _, _, ranks, _ = factors.shape
    half = -(-2 * modes // 128) * 64
    rows = capacity * 2 * ranks
    group = min(n_freq // 2, 4)
    table = jnp.asarray(wave_table(modes, half, samples))
    stays = pl.BlockSpec(memory_space=pltpu.HBM)
    out = pl.pallas_call(
        functools.partial(kernel, (n_freq, n_bl, modes, half, capacity, ranks)),
        out_shape=pltpu.VMEM((2, modes, base_here), BF16),
        in_specs=[stays] * 5,
        out_specs=pl.BlockSpec(memory_space=pltpu.VMEM),
        scratch_shapes=[
            pltpu.VMEM((CHUNKS, 2, base_here, samples // CHUNKS), BF16),
            pltpu.VMEM((samples, 2 * half), BF16),
            pltpu.VMEM((1, modes), jnp.int32),
            pltpu.VMEM((n_freq, modes), jnp.int32),
            pltpu.VMEM((n_freq, capacity, 2, ranks, base_here), BF16),
            pltpu.VMEM((n_freq // group, group * rows, base_here), BF16),
            pltpu.VMEM((n_freq // group, 2 * half, group * rows), BF16),
            pltpu.VMEM((8, 2 * half), F32),
            pltpu.VMEM((8, 2 * half), F32),
            pltpu.VMEM((base_here, 2 * half), BF16),
            pltpu.VMEM((n_bl, 2 * ranks, 2 * half), F32),
            pltpu.SemaphoreType.DMA((CHUNKS,)),
            pltpu.SemaphoreType.DMA((CHUNKS,)),
            pltpu.SemaphoreType.DMA((3,)),
            pltpu.SemaphoreType.DMA((n_freq,)),
            pltpu.SemaphoreType.DMA((n_freq,)),
            pltpu.SemaphoreType.DMA((n_bl,)),
            pltpu.SemaphoreType.DMA((n_bl,)),
        ],
        compiler_params=pltpu.CompilerParams(
            collective_id=0, has_side_effects=True, vmem_limit_bytes=63 * 1024 * 1024
        ),
    )(vis_time, table, owner.T, counts.T, factors)
    return out.transpose(0, 2, 1)[None]


def solution(mesh):
    placed = (P("freq", None, "bl", None), P(), P(), P("freq", None, None, None, "bl"))
    return jax.shard_map(
        functools.partial(local, mesh.shape["freq"], mesh.shape["bl"]),
        mesh=mesh, in_specs=placed, out_specs=P("freq", None, "bl", None), check_vma=False,
    )
```

```python
import functools
import math

import jax
import jax.numpy as jnp
import numpy as np
from jax import lax
from jax.experimental import pallas as pl
from jax.experimental.pallas import tpu as pltpu
from jax.sharding import PartitionSpec as P

NB = 1024
CHUNKS = 2
F32 = jnp.float32
BF16 = jnp.bfloat16
MESH = pl.DeviceIdType.MESH


def wave_table(modes, half, samples):
    times = np.arange(samples, dtype=np.int64)[:, None]
    phases = times * np.arange(modes, dtype=np.int64)[None, :] % samples
    angles = phases * (2.0 * math.pi / samples)
    table = np.zeros((samples, 2 * half), np.float32)
    table[:, :modes] = np.cos(angles) / math.sqrt(samples)
    table[:, half : half + modes] = np.sin(angles) / math.sqrt(samples)
    return table.astype(BF16)


def kernel(
    dims, vis_ref, table_ref, owner_ref, counts_ref, factors_ref, out_ref,
    vis, table, owner, counts, held, packed, spread, slots, limits, spectrum, part,
    vis_sem, table_sem, small_sem, send_sem, recv_sem, part_send, part_recv,
):
    n_freq, n_bl, modes, half, capacity, ranks = dims
    lanes = 2 * half
    rows = capacity * 2 * ranks
    group = max(2, n_freq // 32)
    deep = group * rows
    blocks = n_freq // group
    wide = min(n_freq, 8) * rows
    base_here, step = vis.shape[2], vis.shape[3]
    me = lax.axis_index("freq")
    mine = lax.axis_index("bl")

    def peers(body):
        def turn(k, carry):
            body(k + (k - me + n_freq) // n_freq)
            return carry

        if n_freq <= 8:
            for k in range(n_freq - 1):
                turn(k, 0)
        else:
            lax.fori_loop(0, n_freq - 1, turn, 0)

    barrier = pltpu.get_barrier_semaphore()

    def greet(to):
        pl.semaphore_signal(barrier, inc=1, device_id={"freq": to}, device_id_type=MESH)

    peers(greet)
    for d in range(1, n_bl):
        pl.semaphore_signal(
            barrier, inc=1, device_id={"bl": lax.rem(mine + d, n_bl)}, device_id_type=MESH
        )

    def vis_copy(c):
        return pltpu.make_async_copy(
            vis_ref.at[0, :, :, pl.ds(c * step, step)], vis.at[c], vis_sem.at[c]
        )

    def table_copy(c):
        times = pl.ds(c * step, step)
        return pltpu.make_async_copy(table_ref.at[times], table.at[times], table_sem.at[c])

    owner_copy = pltpu.make_async_copy(owner_ref, owner, small_sem.at[0])
    counts_copy = pltpu.make_async_copy(counts_ref, counts, small_sem.at[1])
    own_copy = pltpu.make_async_copy(factors_ref.at[:, me], held.at[me], small_sem.at[2])

    def fetch():
        for c in range(CHUNKS):
            table_copy(c).start()
            vis_copy(c).start()
        owner_copy.start()
        counts_copy.start()
        own_copy.start()

    def factor_copy(to, source):
        return pltpu.make_async_remote_copy(
            src_ref=factors_ref.at[:, to], dst_ref=held.at[source],
            send_sem=send_sem.at[to], recv_sem=recv_sem.at[source],
            device_id={"freq": to}, device_id_type=MESH,
        )

    def prepare():
        owner_copy.wait()
        counts_copy.wait()
        lane = lax.broadcasted_iota(jnp.int32, (modes, lanes), 1)
        mode = lax.broadcasted_iota(jnp.int32, (modes, lanes), 0)
        spreading = jnp.where(lane % half == mode, 1.0, 0.0).astype(BF16)
        owner_row = jnp.broadcast_to(owner[...] + 1, (8, modes)).astype(F32).astype(BF16)
        owner_lanes = jnp.dot(owner_row, spreading, preferred_element_type=F32)[:1] - 1.0
        counts_row = jnp.broadcast_to(counts[pl.ds(me, 1), :], (8, modes)).astype(F32).astype(BF16)
        limits[...] = jnp.dot(counts_row, spreading, preferred_element_type=F32)
        owner_ids = lax.broadcasted_iota(jnp.int32, (n_freq, lanes), 0).astype(F32)
        onehot = jnp.where(owner_lanes == owner_ids, 1.0, 0.0)
        first = lax.broadcasted_iota(jnp.int32, (lanes, lanes), 0)
        second = lax.broadcasted_iota(jnp.int32, (lanes, lanes), 1)
        earlier = (first < second) & (first // half == second // half)
        earlier = jnp.where(earlier, 1.0, 0.0).astype(BF16)
        before = jnp.dot(onehot.astype(BF16), earlier, preferred_element_type=F32)
        ranking = jnp.sum(before * onehot, axis=0, keepdims=True)
        slot = owner_lanes * capacity + ranking
        slots[...] = jnp.broadcast_to(slot, (8, lanes))
        slot_col = jnp.broadcast_to(slot, (8, lanes)).T[:, :1]
        scale = math.sqrt(NB / ranks)
        for g in range(n_freq * rows // wide):
            col = lax.broadcasted_iota(jnp.int32, (lanes, wide), 1) // (2 * ranks)
            col = (col + g * (wide // (2 * ranks))).astype(F32)
            spread[g] = jnp.where(slot_col == col, scale, 0.0).astype(spread.dtype)

        spectra = jnp.zeros((2 * base_here, lanes), F32)
        for c in range(CHUNKS):
            table_copy(c).wait()
            vis_copy(c).wait()
            spectra = spectra + jnp.dot(
                vis[c].reshape(2 * base_here, step), table[c * step : (c + 1) * step],
                preferred_element_type=F32,
            )
        real, imag = spectra[:base_here], spectra[base_here:]
        low = lax.broadcasted_iota(jnp.int32, (base_here, lanes), 1) < half
        spectrum[...] = (jnp.where(low, real, -real) + pltpu.roll(imag, half, 1)).astype(BF16)

    leading = me < n_freq // 2

    @pl.when(leading)
    def _():
        fetch()
        prepare()

    pl.semaphore_wait(barrier, n_freq - 1 + n_bl - 1)
    peers(lambda to: factor_copy(to, me).start())

    @pl.when(jnp.logical_not(leading))
    def _():
        fetch()
        prepare()

    slot = slots[:1]
    def coefficients(block):
        from_here = pl.ds(block * group, group)
        factor = held[from_here].reshape(deep, base_here)
        packed[pl.ds(pl.multiple_of(block * deep, deep), deep)] = factor
        dense = jnp.dot(factor, spectrum[...], preferred_element_type=F32)
        row = lax.broadcasted_iota(jnp.int32, (deep, lanes), 0) // (2 * ranks)
        row = (row + block * group * capacity).astype(F32)
        chosen = jnp.where(slot == row, dense, 0.0)
        return chosen.reshape(group * capacity, 2 * ranks, lanes).sum(axis=0)

    own_copy.wait()
    total = jnp.zeros((2 * ranks, lanes), F32)
    for b in range(blocks):
        block = lax.rem(me // group + b, blocks)
        for j in range(group if b else group - 1):
            source = block * group + (j if b else (me + 1 + j) % group)
            factor_copy(source, source).wait_recv()
        total = total + coefficients(block)
    rank_row = lax.broadcasted_iota(jnp.int32, (2 * ranks, lanes), 0)
    in_low = lax.broadcasted_iota(jnp.int32, (2 * ranks, lanes), 1) < half
    crossed = pltpu.roll(pltpu.roll(total, ranks, 0), half, 1)
    part[mine] = total + jnp.where(in_low == (rank_row < ranks), crossed, -crossed)

    def part_copy(d, at):
        return pltpu.make_async_remote_copy(
            src_ref=part.at[mine], dst_ref=part.at[at],
            send_sem=part_send.at[d], recv_sem=part_recv.at[d],
            device_id={"bl": lax.rem(mine + d, n_bl)}, device_id_type=MESH,
        )

    for d in range(1, n_bl):
        part_copy(d, mine).start()
    for d in range(1, n_bl):
        part_copy(d, lax.rem(mine + n_bl - d, n_bl)).wait_recv()
    summed = part[0]
    for b in range(1, n_bl):
        summed = summed + part[b]
    kept = jnp.where((rank_row % ranks).astype(F32) < limits[:2 * ranks], summed, 0.0).astype(BF16)

    tiling = lax.broadcasted_iota(jnp.int32, (2 * ranks, wide), 1) % (2 * ranks)
    tiling = jnp.where(
        tiling == lax.broadcasted_iota(jnp.int32, (2 * ranks, wide), 0), 1.0, 0.0
    ).astype(BF16)
    tiled = lax.dot_general(
        kept, tiling, (((0,), (0,)), ((), ())), preferred_element_type=F32
    )
    filtered = jnp.zeros((lanes, base_here), F32)
    for g in range(n_freq * rows // wide):
        weight = (tiled * spread[g].astype(F32)).astype(BF16)
        factor = packed[g * wide : (g + 1) * wide]
        filtered = filtered + jnp.dot(weight, factor, preferred_element_type=F32)
    filtered = filtered.astype(BF16)
    out_ref[0] = filtered[:modes]
    out_ref[1] = filtered[half : half + modes]
    peers(lambda to: factor_copy(to, me).wait_send())
    for d in range(1, n_bl):
        part_copy(d, mine).wait_send()


def local(n_freq, n_bl, vis_time, owner, counts, factors):
    _, _, base_here, samples = vis_time.shape
    modes = owner.shape[0]
    capacity, _, _, ranks, _ = factors.shape
    half = -(-2 * modes // 128) * 64
    rows = capacity * 2 * ranks
    wide = min(n_freq, 8) * rows
    table = jnp.asarray(wave_table(modes, half, samples))
    stays = pl.BlockSpec(memory_space=pltpu.HBM)
    out = pl.pallas_call(
        functools.partial(kernel, (n_freq, n_bl, modes, half, capacity, ranks)),
        out_shape=pltpu.VMEM((2, modes, base_here), BF16),
        in_specs=[stays] * 5,
        out_specs=pl.BlockSpec(memory_space=pltpu.VMEM),
        scratch_shapes=[
            pltpu.VMEM((CHUNKS, 2, base_here, samples // CHUNKS), BF16),
            pltpu.VMEM((samples, 2 * half), BF16),
            pltpu.VMEM((1, modes), jnp.int32),
            pltpu.VMEM((n_freq, modes), jnp.int32),
            pltpu.VMEM((n_freq, capacity, 2, ranks, base_here), BF16),
            pltpu.VMEM((n_freq * rows, base_here), BF16),
            pltpu.VMEM((n_freq * rows // wide, 2 * half, wide), BF16),
            pltpu.VMEM((8, 2 * half), F32),
            pltpu.VMEM((8, 2 * half), F32),
            pltpu.VMEM((base_here, 2 * half), BF16),
            pltpu.VMEM((n_bl, 2 * ranks, 2 * half), F32),
            pltpu.SemaphoreType.DMA((CHUNKS,)),
            pltpu.SemaphoreType.DMA((CHUNKS,)),
            pltpu.SemaphoreType.DMA((3,)),
            pltpu.SemaphoreType.DMA((n_freq,)),
            pltpu.SemaphoreType.DMA((n_freq,)),
            pltpu.SemaphoreType.DMA((n_bl,)),
            pltpu.SemaphoreType.DMA((n_bl,)),
        ],
        compiler_params=pltpu.CompilerParams(
            collective_id=0, has_side_effects=True, vmem_limit_bytes=63 * 1024 * 1024
        ),
    )(vis_time, table, owner.T, counts.T, factors)
    return out.transpose(0, 2, 1)[None]


def solution(mesh):
    placed = (P("freq", None, "bl", None), P(), P(), P("freq", None, None, None, "bl"))
    return jax.shard_map(
        functools.partial(local, mesh.shape["freq"], mesh.shape["bl"]),
        mesh=mesh, in_specs=placed, out_specs=P("freq", None, "bl", None), check_vma=False,
    )
```

```python
import functools
import math

import jax
import jax.numpy as jnp
import numpy as np
from jax import lax
from jax.experimental import pallas as pl
from jax.experimental.pallas import tpu as pltpu
from jax.sharding import PartitionSpec as P

NB = 1024
CHUNKS = 8
F32 = jnp.float32
BF16 = jnp.bfloat16
MESH = pl.DeviceIdType.MESH


def wave_table(modes, half, samples):
    times = np.arange(samples, dtype=np.int64)[:, None]
    phases = times * np.arange(modes, dtype=np.int64)[None, :] % samples
    angles = phases * (2.0 * math.pi / samples)
    table = np.zeros((samples, 2 * half), np.float32)
    table[:, :modes] = np.cos(angles) / math.sqrt(samples)
    table[:, half : half + modes] = np.sin(angles) / math.sqrt(samples)
    return table.astype(BF16)


def kernel(
    dims, vis_ref, table_ref, owner_ref, counts_ref, factors_ref, out_ref,
    vis, table, owner, counts, held, packed, spread, slots, limits, spectra, spectrum, part,
    vis_sem, table_sem, small_sem, send_sem, recv_sem, part_send, part_recv,
):
    n_freq, n_bl, modes, half, capacity, ranks = dims
    lanes = 2 * half
    rows = capacity * 2 * ranks
    group = max(2, n_freq // 32)
    deep = group * rows
    blocks = n_freq // group
    wide = min(n_freq, 8) * rows
    base_here, step = vis.shape[2], vis.shape[3]
    me = lax.axis_index("freq")
    mine = lax.axis_index("bl")

    def peers(body):
        def turn(k, carry):
            body(k + (k - me + n_freq) // n_freq)
            return carry

        lax.fori_loop(0, n_freq - 1, turn, 0)

    barrier = pltpu.get_barrier_semaphore()

    def greet(to):
        pl.semaphore_signal(barrier, inc=1, device_id={"freq": to}, device_id_type=MESH)

    peers(greet)
    for d in range(1, n_bl):
        pl.semaphore_signal(
            barrier, inc=1, device_id={"bl": lax.rem(mine + d, n_bl)}, device_id_type=MESH
        )

    def vis_copy(c):
        return pltpu.make_async_copy(
            vis_ref.at[0, :, :, pl.ds(pl.multiple_of(c * step, step), step)], vis.at[c], vis_sem.at[c]
        )

    def table_copy(c):
        times = pl.ds(pl.multiple_of(c * step, step), step)
        return pltpu.make_async_copy(table_ref.at[times], table.at[times], table_sem.at[c])

    owner_copy = pltpu.make_async_copy(owner_ref, owner, small_sem.at[0])
    counts_copy = pltpu.make_async_copy(counts_ref, counts, small_sem.at[1])
    own_copy = pltpu.make_async_copy(factors_ref.at[:, me], held.at[me], small_sem.at[2])

    def fetch():
        def begin(c, carry):
            table_copy(c).start()
            vis_copy(c).start()
            return carry

        lax.fori_loop(0, CHUNKS, begin, 0)
        owner_copy.start()
        counts_copy.start()
        own_copy.start()

    def factor_copy(to, source):
        return pltpu.make_async_remote_copy(
            src_ref=factors_ref.at[:, to], dst_ref=held.at[source],
            send_sem=send_sem.at[to], recv_sem=recv_sem.at[source],
            device_id={"freq": to}, device_id_type=MESH,
        )

    def prepare():
        owner_copy.wait()
        counts_copy.wait()
        lane = lax.broadcasted_iota(jnp.int32, (modes, lanes), 1)
        mode = lax.broadcasted_iota(jnp.int32, (modes, lanes), 0)
        spreading = jnp.where(lane % half == mode, 1.0, 0.0).astype(BF16)
        owner_row = jnp.broadcast_to(owner[...] + 1, (8, modes)).astype(F32).astype(BF16)
        owner_lanes = jnp.dot(owner_row, spreading, preferred_element_type=F32)[:1] - 1.0
        counts_row = jnp.broadcast_to(counts[pl.ds(me, 1), :], (8, modes)).astype(F32).astype(BF16)
        limits[...] = jnp.dot(counts_row, spreading, preferred_element_type=F32)
        owner_ids = lax.broadcasted_iota(jnp.int32, (n_freq, lanes), 0).astype(F32)
        onehot = jnp.where(owner_lanes == owner_ids, 1.0, 0.0)
        first = lax.broadcasted_iota(jnp.int32, (lanes, lanes), 0)
        second = lax.broadcasted_iota(jnp.int32, (lanes, lanes), 1)
        earlier = (first < second) & (first // half == second // half)
        earlier = jnp.where(earlier, 1.0, 0.0).astype(BF16)
        before = jnp.dot(onehot.astype(BF16), earlier, preferred_element_type=F32)
        ranking = jnp.sum(before * onehot, axis=0, keepdims=True)
        slot = owner_lanes * capacity + ranking
        slots[...] = jnp.broadcast_to(slot, (8, lanes))
        slot_col = jnp.broadcast_to(slot, (8, lanes)).T[:, :1]
        scale = math.sqrt(NB / ranks)
        for g in range(n_freq * rows // wide):
            col = lax.broadcasted_iota(jnp.int32, (lanes, wide), 1) // (2 * ranks)
            col = (col + g * (wide // (2 * ranks))).astype(F32)
            spread[g] = jnp.where(slot_col == col, scale, 0.0).astype(spread.dtype)

        spectra[...] = jnp.zeros_like(spectra)

        def add(c, carry):
            table_copy(c).wait()
            vis_copy(c).wait()
            spectra[...] += jnp.dot(
                vis[c].reshape(2 * base_here, step), table[pl.ds(pl.multiple_of(c * step, step), step)],
                preferred_element_type=F32,
            )
            return carry

        lax.fori_loop(0, CHUNKS, add, 0)
        real, imag = spectra[:base_here], spectra[base_here:]
        low = lax.broadcasted_iota(jnp.int32, (base_here, lanes), 1) < half
        spectrum[...] = (jnp.where(low, real, -real) + pltpu.roll(imag, half, 1)).astype(BF16)

    first_turn = (me * 2) // n_freq

    def phase(turn, carry):
        @pl.when(turn == first_turn)
        def _():
            fetch()
            prepare()

        @pl.when(turn != first_turn)
        def _():
            pl.semaphore_wait(barrier, n_freq - 1 + n_bl - 1)
            peers(lambda to: factor_copy(to, me).start())

        return carry

    lax.fori_loop(0, 2, phase, 0)

    slot = slots[:1]
    def coefficients(block):
        from_here = pl.ds(block * group, group)
        factor = held[from_here].reshape(deep, base_here)
        packed[pl.ds(pl.multiple_of(block * deep, deep), deep)] = factor
        dense = jnp.dot(factor, spectrum[...], preferred_element_type=F32)
        row = lax.broadcasted_iota(jnp.int32, (deep, lanes), 0) // (2 * ranks)
        row = (row + block * group * capacity).astype(F32)
        chosen = jnp.where(slot == row, dense, 0.0)
        return chosen.reshape(group * capacity, 2 * ranks, lanes).sum(axis=0)

    own_copy.wait()

    def arrived(b, total):
        block = lax.rem(me // group + b, blocks)
        for j in range(group):
            source = block * group + j

            @pl.when(source != me)
            def _():
                factor_copy(source, source).wait_recv()

        return total + coefficients(block)

    total = lax.fori_loop(0, blocks, arrived, jnp.zeros((2 * ranks, lanes), F32))
    rank_row = lax.broadcasted_iota(jnp.int32, (2 * ranks, lanes), 0)
    in_low = lax.broadcasted_iota(jnp.int32, (2 * ranks, lanes), 1) < half
    crossed = pltpu.roll(pltpu.roll(total, ranks, 0), half, 1)
    part[mine] = total + jnp.where(in_low == (rank_row < ranks), crossed, -crossed)

    def part_copy(d, at):
        return pltpu.make_async_remote_copy(
            src_ref=part.at[mine], dst_ref=part.at[at],
            send_sem=part_send.at[d], recv_sem=part_recv.at[d],
            device_id={"bl": lax.rem(mine + d, n_bl)}, device_id_type=MESH,
        )

    for d in range(1, n_bl):
        part_copy(d, mine).start()
    for d in range(1, n_bl):
        part_copy(d, lax.rem(mine + n_bl - d, n_bl)).wait_recv()
    summed = part[0]
    for b in range(1, n_bl):
        summed = summed + part[b]
    kept = jnp.where((rank_row % ranks).astype(F32) < limits[:2 * ranks], summed, 0.0).astype(BF16)

    tiling = lax.broadcasted_iota(jnp.int32, (2 * ranks, wide), 1) % (2 * ranks)
    tiling = jnp.where(
        tiling == lax.broadcasted_iota(jnp.int32, (2 * ranks, wide), 0), 1.0, 0.0
    ).astype(BF16)
    tiled = lax.dot_general(
        kept, tiling, (((0,), (0,)), ((), ())), preferred_element_type=F32
    )
    filtered = jnp.zeros((lanes, base_here), F32)
    for g in range(n_freq * rows // wide):
        weight = (tiled * spread[g].astype(F32)).astype(BF16)
        factor = packed[g * wide : (g + 1) * wide]
        filtered = filtered + jnp.dot(weight, factor, preferred_element_type=F32)
    filtered = filtered.astype(BF16)
    out_ref[0] = filtered[:modes]
    out_ref[1] = filtered[half : half + modes]
    peers(lambda to: factor_copy(to, me).wait_send())
    for d in range(1, n_bl):
        part_copy(d, mine).wait_send()


def local(n_freq, n_bl, vis_time, owner, counts, factors):
    _, _, base_here, samples = vis_time.shape
    modes = owner.shape[0]
    capacity, _, _, ranks, _ = factors.shape
    half = -(-2 * modes // 128) * 64
    rows = capacity * 2 * ranks
    wide = min(n_freq, 8) * rows
    table = jnp.asarray(wave_table(modes, half, samples))
    stays = pl.BlockSpec(memory_space=pltpu.HBM)
    out = pl.pallas_call(
        functools.partial(kernel, (n_freq, n_bl, modes, half, capacity, ranks)),
        out_shape=pltpu.VMEM((2, modes, base_here), BF16),
        in_specs=[stays] * 5,
        out_specs=pl.BlockSpec(memory_space=pltpu.VMEM),
        scratch_shapes=[
            pltpu.VMEM((CHUNKS, 2, base_here, samples // CHUNKS), BF16),
            pltpu.VMEM((samples, 2 * half), BF16),
            pltpu.VMEM((1, modes), jnp.int32),
            pltpu.VMEM((n_freq, modes), jnp.int32),
            pltpu.VMEM((n_freq, capacity, 2, ranks, base_here), BF16),
            pltpu.VMEM((n_freq * rows, base_here), BF16),
            pltpu.VMEM((n_freq * rows // wide, 2 * half, wide), BF16),
            pltpu.VMEM((8, 2 * half), F32),
            pltpu.VMEM((8, 2 * half), F32),
            pltpu.VMEM((2 * base_here, 2 * half), F32),
            pltpu.VMEM((base_here, 2 * half), BF16),
            pltpu.VMEM((n_bl, 2 * ranks, 2 * half), F32),
            pltpu.SemaphoreType.DMA((CHUNKS,)),
            pltpu.SemaphoreType.DMA((CHUNKS,)),
            pltpu.SemaphoreType.DMA((3,)),
            pltpu.SemaphoreType.DMA((n_freq,)),
            pltpu.SemaphoreType.DMA((n_freq,)),
            pltpu.SemaphoreType.DMA((n_bl,)),
            pltpu.SemaphoreType.DMA((n_bl,)),
        ],
        compiler_params=pltpu.CompilerParams(
            collective_id=0, has_side_effects=True, vmem_limit_bytes=63 * 1024 * 1024
        ),
    )(vis_time, table, owner.T, counts.T, factors)
    return out.transpose(0, 2, 1)[None]


def solution(mesh):
    placed = (P("freq", None, "bl", None), P(), P(), P("freq", None, None, None, "bl"))
    return jax.shard_map(
        functools.partial(local, mesh.shape["freq"], mesh.shape["bl"]),
        mesh=mesh, in_specs=placed, out_specs=P("freq", None, "bl", None), check_vma=False,
    )
```

```python
import functools
import math

import jax
import jax.numpy as jnp
import numpy as np
from jax import lax
from jax.experimental import pallas as pl
from jax.experimental.pallas import tpu as pltpu
from jax.sharding import PartitionSpec as P

NB = 1024
CHUNKS = 2
F32 = jnp.float32
BF16 = jnp.bfloat16
MESH = pl.DeviceIdType.MESH


def wave_table(modes, half, samples):
    times = np.arange(samples, dtype=np.int64)[:, None]
    phases = times * np.arange(modes, dtype=np.int64)[None, :] % samples
    angles = phases * (2.0 * math.pi / samples)
    table = np.zeros((samples, 2 * half), np.float32)
    table[:, :modes] = np.cos(angles) / math.sqrt(samples)
    table[:, half : half + modes] = np.sin(angles) / math.sqrt(samples)
    return table.astype(BF16)


def kernel(
    dims, vis_ref, table_ref, owner_ref, counts_ref, factors_ref, out_ref,
    vis, table, owner, counts, held, packed, spread, slots, limits, spectrum, part,
    vis_sem, table_sem, small_sem, send_sem, recv_sem, part_send, part_recv,
):
    n_freq, n_bl, modes, half, capacity, ranks = dims
    lanes = 2 * half
    rows = capacity * 2 * ranks
    group = max(2, n_freq // 32)
    deep = group * rows
    blocks = n_freq // group
    wide = min(n_freq, 8) * rows
    base_here, step = vis.shape[2], vis.shape[3]
    me = lax.axis_index("freq")
    mine = lax.axis_index("bl")

    def others(count, own, body):
        def turn(k, carry):
            @pl.when(k != own)
            def _():
                body(k)

            return carry

        if count <= 8:
            for k in range(count):
                turn(k, 0)
        else:
            lax.fori_loop(0, count, turn, 0)

    def peers(body):
        others(n_freq, me, body)

    def partners(body):
        others(n_bl, mine, body)

    barrier = pltpu.get_barrier_semaphore()

    def greet(to):
        pl.semaphore_signal(barrier, inc=1, device_id={"freq": to}, device_id_type=MESH)

    peers(greet)

    def greet_partner(to):
        pl.semaphore_signal(barrier, inc=1, device_id={"bl": to}, device_id_type=MESH)

    partners(greet_partner)

    def vis_copy(c):
        return pltpu.make_async_copy(
            vis_ref.at[0, :, :, pl.ds(c * step, step)], vis.at[c], vis_sem.at[c]
        )

    def table_copy(c):
        times = pl.ds(c * step, step)
        return pltpu.make_async_copy(table_ref.at[times], table.at[times], table_sem.at[c])

    owner_copy = pltpu.make_async_copy(owner_ref, owner, small_sem.at[0])
    counts_copy = pltpu.make_async_copy(counts_ref, counts, small_sem.at[1])
    own_copy = pltpu.make_async_copy(factors_ref.at[:, me], held.at[me], small_sem.at[2])

    def fetch():
        for c in range(CHUNKS):
            table_copy(c).start()
            vis_copy(c).start()
        owner_copy.start()
        counts_copy.start()
        own_copy.start()

    def factor_copy(to, source):
        return pltpu.make_async_remote_copy(
            src_ref=factors_ref.at[:, to], dst_ref=held.at[source],
            send_sem=send_sem.at[to], recv_sem=recv_sem.at[source],
            device_id={"freq": to}, device_id_type=MESH,
        )

    def prepare():
        owner_copy.wait()
        counts_copy.wait()
        lane = lax.broadcasted_iota(jnp.int32, (modes, lanes), 1)
        mode = lax.broadcasted_iota(jnp.int32, (modes, lanes), 0)
        spreading = jnp.where(lane % half == mode, 1.0, 0.0).astype(BF16)
        owner_row = jnp.broadcast_to(owner[...] + 1, (8, modes)).astype(F32).astype(BF16)
        owner_lanes = jnp.dot(owner_row, spreading, preferred_element_type=F32)[:1] - 1.0
        counts_row = jnp.broadcast_to(counts[pl.ds(me, 1), :], (8, modes)).astype(F32).astype(BF16)
        limits[...] = jnp.dot(counts_row, spreading, preferred_element_type=F32)
        owner_ids = lax.broadcasted_iota(jnp.int32, (n_freq, lanes), 0).astype(F32)
        onehot = jnp.where(owner_lanes == owner_ids, 1.0, 0.0)
        first = lax.broadcasted_iota(jnp.int32, (lanes, lanes), 0)
        second = lax.broadcasted_iota(jnp.int32, (lanes, lanes), 1)
        earlier = (first < second) & (first // half == second // half)
        earlier = jnp.where(earlier, 1.0, 0.0).astype(BF16)
        before = jnp.dot(onehot.astype(BF16), earlier, preferred_element_type=F32)
        ranking = jnp.sum(before * onehot, axis=0, keepdims=True)
        slot = owner_lanes * capacity + ranking
        slots[...] = jnp.broadcast_to(slot, (8, lanes))
        slot_col = jnp.broadcast_to(slot, (8, lanes)).T[:, :1]
        scale = math.sqrt(NB / ranks)
        for g in range(n_freq * rows // wide):
            col = lax.broadcasted_iota(jnp.int32, (lanes, wide), 1) // (2 * ranks)
            col = (col + g * (wide // (2 * ranks))).astype(F32)
            spread[g] = jnp.where(slot_col == col, scale, 0.0).astype(spread.dtype)

        spectra = jnp.zeros((2 * base_here, lanes), F32)
        for c in range(CHUNKS):
            table_copy(c).wait()
            vis_copy(c).wait()
            spectra = spectra + jnp.dot(
                vis[c].reshape(2 * base_here, step), table[c * step : (c + 1) * step],
                preferred_element_type=F32,
            )
        real, imag = spectra[:base_here], spectra[base_here:]
        low = lax.broadcasted_iota(jnp.int32, (base_here, lanes), 1) < half
        spectrum[...] = (jnp.where(low, real, -real) + pltpu.roll(imag, half, 1)).astype(BF16)

    leading = me < n_freq // 2

    @pl.when(leading)
    def _():
        fetch()
        prepare()

    pl.semaphore_wait(barrier, n_freq - 1 + n_bl - 1)
    peers(lambda to: factor_copy(to, me).start())

    @pl.when(jnp.logical_not(leading))
    def _():
        fetch()
        prepare()

    slot = slots[:1]
    def coefficients(block):
        factor = held[block * group : (block + 1) * group].reshape(deep, base_here)
        packed[block * deep : (block + 1) * deep] = factor
        dense = jnp.dot(factor, spectrum[...], preferred_element_type=F32)
        row = lax.broadcasted_iota(jnp.int32, (deep, lanes), 0) // (2 * ranks)
        row = (row + block * group * capacity).astype(F32)
        chosen = jnp.where(slot == row, dense, 0.0)
        return chosen.reshape(group * capacity, 2 * ranks, lanes).sum(axis=0)

    own_copy.wait()
    total = jnp.zeros((2 * ranks, lanes), F32)
    for block in range(blocks):
        for j in range(group):
            source = block * group + j

            @pl.when(source != me)
            def _():
                factor_copy(source, source).wait_recv()

        total = total + coefficients(block)
    rank_row = lax.broadcasted_iota(jnp.int32, (2 * ranks, lanes), 0)
    in_low = lax.broadcasted_iota(jnp.int32, (2 * ranks, lanes), 1) < half
    crossed = pltpu.roll(pltpu.roll(total, ranks, 0), half, 1)
    part[mine] = total + jnp.where(in_low == (rank_row < ranks), crossed, -crossed)

    def part_copy(to, source):
        return pltpu.make_async_remote_copy(
            src_ref=part.at[mine], dst_ref=part.at[source],
            send_sem=part_send.at[to], recv_sem=part_recv.at[source],
            device_id={"bl": to}, device_id_type=MESH,
        )

    partners(lambda to: part_copy(to, mine).start())
    peers(lambda to: factor_copy(to, me).wait_send())
    partners(lambda source: part_copy(source, source).wait_recv())
    summed = part[0]
    for b in range(1, n_bl):
        summed = summed + part[b]
    kept = jnp.where((rank_row % ranks).astype(F32) < limits[:2 * ranks], summed, 0.0).astype(BF16)

    tiling = lax.broadcasted_iota(jnp.int32, (2 * ranks, wide), 1) % (2 * ranks)
    tiling = jnp.where(
        tiling == lax.broadcasted_iota(jnp.int32, (2 * ranks, wide), 0), 1.0, 0.0
    ).astype(BF16)
    tiled = lax.dot_general(
        kept, tiling, (((0,), (0,)), ((), ())), preferred_element_type=F32
    )
    filtered = jnp.zeros((lanes, base_here), F32)
    for g in range(n_freq * rows // wide):
        weight = (tiled * spread[g].astype(F32)).astype(BF16)
        factor = packed[g * wide : (g + 1) * wide]
        filtered = filtered + jnp.dot(weight, factor, preferred_element_type=F32)
    filtered = filtered.astype(BF16)
    out_ref[0] = filtered[:modes]
    out_ref[1] = filtered[half : half + modes]
    partners(lambda to: part_copy(to, mine).wait_send())


def local(n_freq, n_bl, vis_time, owner, counts, factors):
    _, _, base_here, samples = vis_time.shape
    modes = owner.shape[0]
    capacity, _, _, ranks, _ = factors.shape
    half = -(-2 * modes // 128) * 64
    rows = capacity * 2 * ranks
    wide = min(n_freq, 8) * rows
    table = jnp.asarray(wave_table(modes, half, samples))
    stays = pl.BlockSpec(memory_space=pltpu.HBM)
    out = pl.pallas_call(
        functools.partial(kernel, (n_freq, n_bl, modes, half, capacity, ranks)),
        out_shape=pltpu.VMEM((2, modes, base_here), BF16),
        in_specs=[stays] * 5,
        out_specs=pl.BlockSpec(memory_space=pltpu.VMEM),
        scratch_shapes=[
            pltpu.VMEM((CHUNKS, 2, base_here, samples // CHUNKS), BF16),
            pltpu.VMEM((samples, 2 * half), BF16),
            pltpu.VMEM((1, modes), jnp.int32),
            pltpu.VMEM((n_freq, modes), jnp.int32),
            pltpu.VMEM((n_freq, capacity, 2, ranks, base_here), BF16),
            pltpu.VMEM((n_freq * rows, base_here), BF16),
            pltpu.VMEM((n_freq * rows // wide, 2 * half, wide), BF16),
            pltpu.VMEM((8, 2 * half), F32),
            pltpu.VMEM((8, 2 * half), F32),
            pltpu.VMEM((base_here, 2 * half), BF16),
            pltpu.VMEM((n_bl, 2 * ranks, 2 * half), F32),
            pltpu.SemaphoreType.DMA((CHUNKS,)),
            pltpu.SemaphoreType.DMA((CHUNKS,)),
            pltpu.SemaphoreType.DMA((3,)),
            pltpu.SemaphoreType.DMA((n_freq,)),
            pltpu.SemaphoreType.DMA((n_freq,)),
            pltpu.SemaphoreType.DMA((n_bl,)),
            pltpu.SemaphoreType.DMA((n_bl,)),
        ],
        compiler_params=pltpu.CompilerParams(
            collective_id=0, has_side_effects=True, vmem_limit_bytes=63 * 1024 * 1024
        ),
    )(vis_time, table, owner.T, counts.T, factors)
    return out.transpose(0, 2, 1)[None]


def solution(mesh):
    placed = (P("freq", None, "bl", None), P(), P(), P("freq", None, None, None, "bl"))
    return jax.shard_map(
        functools.partial(local, mesh.shape["freq"], mesh.shape["bl"]),
        mesh=mesh, in_specs=placed, out_specs=P("freq", None, "bl", None), check_vma=False,
    )
```

```python
import functools
import math

import jax
import jax.numpy as jnp
import numpy as np
from jax import lax
from jax.experimental import pallas as pl
from jax.experimental.pallas import tpu as pltpu
from jax.sharding import PartitionSpec as P

NB = 1024
CHUNKS = 2
F32 = jnp.float32
BF16 = jnp.bfloat16
MESH = pl.DeviceIdType.MESH


def wave_table(modes, half, samples):
    times = np.arange(samples, dtype=np.int64)[:, None]
    phases = times * np.arange(modes, dtype=np.int64)[None, :] % samples
    angles = phases * (2.0 * math.pi / samples)
    table = np.zeros((samples, 2 * half), np.float32)
    table[:, :modes] = np.cos(angles) / math.sqrt(samples)
    table[:, half : half + modes] = np.sin(angles) / math.sqrt(samples)
    return table.astype(BF16)


def kernel(
    dims, vis_ref, table_ref, owner_ref, counts_ref, factors_ref, out_ref,
    vis, table, owner, counts, held, packed, spread, slots, limits, spectrum, part,
    vis_sem, table_sem, small_sem, send_sem, recv_sem, part_send, part_recv,
):
    n_freq, n_bl, modes, half, capacity, ranks = dims
    lanes = 2 * half
    rows = capacity * 2 * ranks
    group = max(2, n_freq // 32)
    deep = group * rows
    blocks = n_freq // group
    wide = min(n_freq, 8) * rows
    base_here, step = vis.shape[2], vis.shape[3]
    me = lax.axis_index("freq")
    mine = lax.axis_index("bl")

    def others(count, own, body, order=None):
        def turn(k, carry):
            @pl.when(k != own)
            def _():
                body(k)

            return carry

        if count <= 8:
            for k in order or range(count):
                turn(k, 0)
        else:
            lax.fori_loop(0, count, turn, 0)

    def peers(body):
        others(n_freq, me, body)

    def partners(body):
        others(n_bl, mine, body)

    barrier = pltpu.get_barrier_semaphore()

    def greet(to):
        pl.semaphore_signal(barrier, inc=1, device_id={"freq": to}, device_id_type=MESH)

    def greet_partner(to):
        pl.semaphore_signal(barrier, inc=1, device_id={"bl": to}, device_id_type=MESH)

    partners(greet_partner)
    others(n_freq, me, greet, range(n_freq - 1, -1, -1))

    def vis_copy(c):
        return pltpu.make_async_copy(
            vis_ref.at[0, :, :, pl.ds(c * step, step)], vis.at[c], vis_sem.at[c]
        )

    def table_copy(c):
        times = pl.ds(c * step, step)
        return pltpu.make_async_copy(table_ref.at[times], table.at[times], table_sem.at[c])

    owner_copy = pltpu.make_async_copy(owner_ref, owner, small_sem.at[0])
    counts_copy = pltpu.make_async_copy(counts_ref, counts, small_sem.at[1])
    own_copy = pltpu.make_async_copy(factors_ref.at[:, me], held.at[me], small_sem.at[2])

    def fetch():
        for c in range(CHUNKS):
            table_copy(c).start()
            vis_copy(c).start()
        owner_copy.start()
        counts_copy.start()
        own_copy.start()

    def factor_copy(to, source):
        return pltpu.make_async_remote_copy(
            src_ref=factors_ref.at[:, to], dst_ref=held.at[source],
            send_sem=send_sem.at[to], recv_sem=recv_sem.at[source],
            device_id={"freq": to}, device_id_type=MESH,
        )

    def used(rows_of_lanes):
        return jnp.concatenate([rows_of_lanes[:modes], rows_of_lanes[half : half + modes]], axis=0)

    def prepare():
        owner_copy.wait()
        counts_copy.wait()
        lane = lax.broadcasted_iota(jnp.int32, (modes, lanes), 1)
        mode = lax.broadcasted_iota(jnp.int32, (modes, lanes), 0)
        spreading = jnp.where(lane % half == mode, 1.0, 0.0).astype(BF16)
        owner_row = jnp.broadcast_to(owner[...] + 1, (8, modes)).astype(F32).astype(BF16)
        owner_lanes = jnp.dot(owner_row, spreading, preferred_element_type=F32)[:1] - 1.0
        counts_row = jnp.broadcast_to(counts[pl.ds(me, 1), :], (8, modes)).astype(F32).astype(BF16)
        limits[...] = jnp.dot(counts_row, spreading, preferred_element_type=F32)
        owner_ids = lax.broadcasted_iota(jnp.int32, (n_freq, lanes), 0).astype(F32)
        onehot = jnp.where(owner_lanes == owner_ids, 1.0, 0.0)
        first = lax.broadcasted_iota(jnp.int32, (lanes, lanes), 0)
        second = lax.broadcasted_iota(jnp.int32, (lanes, lanes), 1)
        earlier = (first < second) & (first // half == second // half)
        earlier = jnp.where(earlier, 1.0, 0.0).astype(BF16)
        before = jnp.dot(onehot.astype(BF16), earlier, preferred_element_type=F32)
        ranking = jnp.sum(before * onehot, axis=0, keepdims=True)
        slot = owner_lanes * capacity + ranking
        slots[...] = jnp.broadcast_to(slot, (8, lanes))
        slot_col = used(jnp.broadcast_to(slot, (8, lanes)).T)[:, :1]
        scale = math.sqrt(NB / ranks)
        for g in range(n_freq * rows // wide):
            col = lax.broadcasted_iota(jnp.int32, (2 * modes, wide), 1) // (2 * ranks)
            col = (col + g * (wide // (2 * ranks))).astype(F32)
            spread[g] = jnp.where(slot_col == col, scale, 0.0).astype(spread.dtype)

        spectra = jnp.zeros((2 * base_here, lanes), F32)
        for c in range(CHUNKS):
            table_copy(c).wait()
            vis_copy(c).wait()
            spectra = spectra + jnp.dot(
                vis[c].reshape(2 * base_here, step), table[c * step : (c + 1) * step],
                preferred_element_type=F32,
            )
        real, imag = spectra[:base_here], spectra[base_here:]
        low = lax.broadcasted_iota(jnp.int32, (base_here, lanes), 1) < half
        spectrum[...] = (jnp.where(low, real, -real) + pltpu.roll(imag, half, 1)).astype(BF16)

    leading = me < n_freq // 2

    @pl.when(leading)
    def _():
        fetch()
        prepare()

    pl.semaphore_wait(barrier, n_freq - 1 + n_bl - 1)
    peers(lambda to: factor_copy(to, me).start())

    @pl.when(jnp.logical_not(leading))
    def _():
        fetch()
        prepare()

    slot = slots[:1]
    def coefficients(block):
        factor = held[block * group : (block + 1) * group].reshape(deep, base_here)
        packed[block * deep : (block + 1) * deep] = factor
        dense = jnp.dot(factor, spectrum[...], preferred_element_type=F32)
        row = lax.broadcasted_iota(jnp.int32, (deep, lanes), 0) // (2 * ranks)
        row = (row + block * group * capacity).astype(F32)
        chosen = jnp.where(slot == row, dense, 0.0)
        return chosen.reshape(group * capacity, 2 * ranks, lanes).sum(axis=0)

    own_copy.wait()
    total = jnp.zeros((2 * ranks, lanes), F32)
    for block in range(blocks):
        for j in range(group):
            source = block * group + j

            @pl.when(source != me)
            def _():
                factor_copy(source, source).wait_recv()

        total = total + coefficients(block)
    rank_row = lax.broadcasted_iota(jnp.int32, (2 * ranks, lanes), 0)
    in_low = lax.broadcasted_iota(jnp.int32, (2 * ranks, lanes), 1) < half
    crossed = pltpu.roll(pltpu.roll(total, ranks, 0), half, 1)
    part[mine] = total + jnp.where(in_low == (rank_row < ranks), crossed, -crossed)

    def part_copy(to, source):
        return pltpu.make_async_remote_copy(
            src_ref=part.at[mine], dst_ref=part.at[source],
            send_sem=part_send.at[to], recv_sem=part_recv.at[source],
            device_id={"bl": to}, device_id_type=MESH,
        )

    partners(lambda to: part_copy(to, mine).start())
    peers(lambda to: factor_copy(to, me).wait_send())
    partners(lambda source: part_copy(source, source).wait_recv())
    summed = part[0]
    for b in range(1, n_bl):
        summed = summed + part[b]
    kept = jnp.where((rank_row % ranks).astype(F32) < limits[:2 * ranks], summed, 0.0).astype(BF16)

    tiling = lax.broadcasted_iota(jnp.int32, (2 * ranks, wide), 1) % (2 * ranks)
    tiling = jnp.where(
        tiling == lax.broadcasted_iota(jnp.int32, (2 * ranks, wide), 0), 1.0, 0.0
    ).astype(BF16)
    tiled = used(lax.dot_general(
        kept, tiling, (((0,), (0,)), ((), ())), preferred_element_type=F32
    ))
    filtered = jnp.zeros((2 * modes, base_here), F32)
    for g in range(n_freq * rows // wide):
        weight = (tiled * spread[g].astype(F32)).astype(BF16)
        factor = packed[g * wide : (g + 1) * wide]
        filtered = filtered + jnp.dot(weight, factor, preferred_element_type=F32)
    filtered = filtered.astype(BF16)
    out_ref[0] = filtered[:modes]
    out_ref[1] = filtered[modes:]
    partners(lambda to: part_copy(to, mine).wait_send())


def local(n_freq, n_bl, vis_time, owner, counts, factors):
    _, _, base_here, samples = vis_time.shape
    modes = owner.shape[0]
    capacity, _, _, ranks, _ = factors.shape
    half = -(-2 * modes // 128) * 64
    rows = capacity * 2 * ranks
    wide = min(n_freq, 8) * rows
    table = jnp.asarray(wave_table(modes, half, samples))
    stays = pl.BlockSpec(memory_space=pltpu.HBM)
    out = pl.pallas_call(
        functools.partial(kernel, (n_freq, n_bl, modes, half, capacity, ranks)),
        out_shape=pltpu.VMEM((2, modes, base_here), BF16),
        in_specs=[stays] * 5,
        out_specs=pl.BlockSpec(memory_space=pltpu.VMEM),
        scratch_shapes=[
            pltpu.VMEM((CHUNKS, 2, base_here, samples // CHUNKS), BF16),
            pltpu.VMEM((samples, 2 * half), BF16),
            pltpu.VMEM((1, modes), jnp.int32),
            pltpu.VMEM((n_freq, modes), jnp.int32),
            pltpu.VMEM((n_freq, capacity, 2, ranks, base_here), BF16),
            pltpu.VMEM((n_freq * rows, base_here), BF16),
            pltpu.VMEM((n_freq * rows // wide, 2 * modes, wide), BF16),
            pltpu.VMEM((8, 2 * half), F32),
            pltpu.VMEM((8, 2 * half), F32),
            pltpu.VMEM((base_here, 2 * half), BF16),
            pltpu.VMEM((n_bl, 2 * ranks, 2 * half), F32),
            pltpu.SemaphoreType.DMA((CHUNKS,)),
            pltpu.SemaphoreType.DMA((CHUNKS,)),
            pltpu.SemaphoreType.DMA((3,)),
            pltpu.SemaphoreType.DMA((n_freq,)),
            pltpu.SemaphoreType.DMA((n_freq,)),
            pltpu.SemaphoreType.DMA((n_bl,)),
            pltpu.SemaphoreType.DMA((n_bl,)),
        ],
        compiler_params=pltpu.CompilerParams(
            collective_id=0, has_side_effects=True, vmem_limit_bytes=63 * 1024 * 1024
        ),
    )(vis_time, table, owner.T, counts.T, factors)
    return out.transpose(0, 2, 1)[None]


def solution(mesh):
    placed = (P("freq", None, "bl", None), P(), P(), P("freq", None, None, None, "bl"))
    return jax.shard_map(
        functools.partial(local, mesh.shape["freq"], mesh.shape["bl"]),
        mesh=mesh, in_specs=placed, out_specs=P("freq", None, "bl", None), check_vma=False,
    )
```

```python
import functools
import math

import jax
import jax.numpy as jnp
import numpy as np
from jax import lax
from jax.experimental import pallas as pl
from jax.experimental.pallas import tpu as pltpu
from jax.sharding import PartitionSpec as P

NB = 1024
CHUNKS = 2
F32 = jnp.float32
BF16 = jnp.bfloat16
MESH = pl.DeviceIdType.MESH


def wave_table(modes, half, samples):
    times = np.arange(samples, dtype=np.int64)[:, None]
    phases = times * np.arange(modes, dtype=np.int64)[None, :] % samples
    angles = phases * (2.0 * math.pi / samples)
    table = np.zeros((samples, 2 * half), np.float32)
    table[:, :modes] = np.cos(angles) / math.sqrt(samples)
    table[:, half : half + modes] = np.sin(angles) / math.sqrt(samples)
    return table.astype(BF16)


def kernel(
    dims, vis_ref, table_ref, owner_ref, counts_ref, factors_ref, out_ref,
    vis, table, owner, counts, held, packed, spread, slots, limits, spectrum, part,
    vis_sem, table_sem, small_sem, send_sem, recv_sem, part_send, part_recv,
):
    n_freq, n_bl, modes, half, capacity, ranks = dims
    lanes = 2 * half
    rows = capacity * 2 * ranks
    group = max(2, n_freq // 32)
    deep = group * rows
    blocks = n_freq // group
    wide = min(n_freq, 8) * rows
    base_here, step = vis.shape[2], vis.shape[3]
    me = lax.axis_index("freq")
    mine = lax.axis_index("bl")

    def others(count, own, body):
        def turn(k, carry):
            @pl.when(k != own)
            def _():
                body(k)

            return carry

        if count <= 8:
            for k in range(count):
                turn(k, 0)
        else:
            lax.fori_loop(0, count, turn, 0)

    def peers(body):
        others(n_freq, me, body)

    def partners(body):
        others(n_bl, mine, body)

    barrier = pltpu.get_barrier_semaphore()

    def greet(to):
        pl.semaphore_signal(barrier, inc=1, device_id={"freq": to}, device_id_type=MESH)

    peers(greet)

    def greet_partner(to):
        pl.semaphore_signal(barrier, inc=1, device_id={"bl": to}, device_id_type=MESH)

    partners(greet_partner)

    def vis_copy(c):
        return pltpu.make_async_copy(
            vis_ref.at[0, :, :, pl.ds(c * step, step)], vis.at[c], vis_sem.at[c]
        )

    def table_copy(c):
        times = pl.ds(c * step, step)
        return pltpu.make_async_copy(table_ref.at[times], table.at[times], table_sem.at[c])

    owner_copy = pltpu.make_async_copy(owner_ref, owner, small_sem.at[0])
    counts_copy = pltpu.make_async_copy(counts_ref, counts, small_sem.at[1])
    own_copy = pltpu.make_async_copy(factors_ref.at[:, me], held.at[me], small_sem.at[2])

    def fetch_small():
        owner_copy.start()
        counts_copy.start()
        own_copy.start()

    def fetch():
        for c in range(CHUNKS):
            table_copy(c).start()
            vis_copy(c).start()

    def factor_copy(to, source):
        return pltpu.make_async_remote_copy(
            src_ref=factors_ref.at[:, to], dst_ref=held.at[source],
            send_sem=send_sem.at[to], recv_sem=recv_sem.at[source],
            device_id={"freq": to}, device_id_type=MESH,
        )

    def prepare():
        owner_copy.wait()
        counts_copy.wait()
        lane = lax.broadcasted_iota(jnp.int32, (modes, lanes), 1)
        mode = lax.broadcasted_iota(jnp.int32, (modes, lanes), 0)
        spreading = jnp.where(lane % half == mode, 1.0, 0.0).astype(BF16)
        owner_row = jnp.broadcast_to(owner[...] + 1, (8, modes)).astype(F32).astype(BF16)
        owner_lanes = jnp.dot(owner_row, spreading, preferred_element_type=F32)[:1] - 1.0
        counts_row = jnp.broadcast_to(counts[pl.ds(me, 1), :], (8, modes)).astype(F32).astype(BF16)
        limits[...] = jnp.dot(counts_row, spreading, preferred_element_type=F32)
        owner_ids = lax.broadcasted_iota(jnp.int32, (n_freq, lanes), 0).astype(F32)
        onehot = jnp.where(owner_lanes == owner_ids, 1.0, 0.0)
        first = lax.broadcasted_iota(jnp.int32, (lanes, lanes), 0)
        second = lax.broadcasted_iota(jnp.int32, (lanes, lanes), 1)
        earlier = (first < second) & (first // half == second // half)
        earlier = jnp.where(earlier, 1.0, 0.0).astype(BF16)
        before = jnp.dot(onehot.astype(BF16), earlier, preferred_element_type=F32)
        ranking = jnp.sum(before * onehot, axis=0, keepdims=True)
        slot = owner_lanes * capacity + ranking
        slots[...] = jnp.broadcast_to(slot, (8, lanes))
        slot_col = jnp.broadcast_to(slot, (8, lanes)).T[:, :1]
        scale = math.sqrt(NB / ranks)
        for g in range(n_freq * rows // wide):
            col = lax.broadcasted_iota(jnp.int32, (lanes, wide), 1) // (2 * ranks)
            col = (col + g * (wide // (2 * ranks))).astype(F32)
            spread[g] = jnp.where(slot_col == col, scale, 0.0).astype(spread.dtype)

        spectra = jnp.zeros((2 * base_here, lanes), F32)
        for c in range(CHUNKS):
            table_copy(c).wait()
            vis_copy(c).wait()
            spectra = spectra + jnp.dot(
                vis[c].reshape(2 * base_here, step), table[c * step : (c + 1) * step],
                preferred_element_type=F32,
            )
        real, imag = spectra[:base_here], spectra[base_here:]
        low = lax.broadcasted_iota(jnp.int32, (base_here, lanes), 1) < half
        spectrum[...] = (jnp.where(low, real, -real) + pltpu.roll(imag, half, 1)).astype(BF16)

    leading = me < n_freq // 2

    @pl.when(leading)
    def _():
        fetch()
        fetch_small()
        prepare()

    pl.semaphore_wait(barrier, n_freq - 1 + n_bl - 1)
    peers(lambda to: factor_copy(to, me).start())

    @pl.when(jnp.logical_not(leading))
    def _():
        fetch_small()
        for k in range(n_freq // 2):
            factor_copy(k, me).wait_send()
        fetch()
        prepare()

    slot = slots[:1]
    def coefficients(block):
        factor = held[block * group : (block + 1) * group].reshape(deep, base_here)
        packed[block * deep : (block + 1) * deep] = factor
        dense = jnp.dot(factor, spectrum[...], preferred_element_type=F32)
        row = lax.broadcasted_iota(jnp.int32, (deep, lanes), 0) // (2 * ranks)
        row = (row + block * group * capacity).astype(F32)
        chosen = jnp.where(slot == row, dense, 0.0)
        return chosen.reshape(group * capacity, 2 * ranks, lanes).sum(axis=0)

    own_copy.wait()
    total = jnp.zeros((2 * ranks, lanes), F32)
    for block in range(blocks):
        for j in range(group):
            source = block * group + j

            @pl.when(source != me)
            def _():
                factor_copy(source, source).wait_recv()

        total = total + coefficients(block)
    rank_row = lax.broadcasted_iota(jnp.int32, (2 * ranks, lanes), 0)
    in_low = lax.broadcasted_iota(jnp.int32, (2 * ranks, lanes), 1) < half
    crossed = pltpu.roll(pltpu.roll(total, ranks, 0), half, 1)
    part[mine] = total + jnp.where(in_low == (rank_row < ranks), crossed, -crossed)

    def part_copy(to, source):
        return pltpu.make_async_remote_copy(
            src_ref=part.at[mine], dst_ref=part.at[source],
            send_sem=part_send.at[to], recv_sem=part_recv.at[source],
            device_id={"bl": to}, device_id_type=MESH,
        )

    partners(lambda to: part_copy(to, mine).start())
    for k in range(n_freq):
        @pl.when((k != me) & (leading if k < n_freq // 2 else True))
        def _():
            factor_copy(k, me).wait_send()

    partners(lambda source: part_copy(source, source).wait_recv())
    summed = part[0]
    for b in range(1, n_bl):
        summed = summed + part[b]
    kept = jnp.where((rank_row % ranks).astype(F32) < limits[:2 * ranks], summed, 0.0).astype(BF16)

    tiling = lax.broadcasted_iota(jnp.int32, (2 * ranks, wide), 1) % (2 * ranks)
    tiling = jnp.where(
        tiling == lax.broadcasted_iota(jnp.int32, (2 * ranks, wide), 0), 1.0, 0.0
    ).astype(BF16)
    tiled = lax.dot_general(
        kept, tiling, (((0,), (0,)), ((), ())), preferred_element_type=F32
    )
    filtered = jnp.zeros((lanes, base_here), F32)
    for g in range(n_freq * rows // wide):
        weight = (tiled * spread[g].astype(F32)).astype(BF16)
        factor = packed[g * wide : (g + 1) * wide]
        filtered = filtered + jnp.dot(weight, factor, preferred_element_type=F32)
    filtered = filtered.astype(BF16)
    out_ref[0] = filtered[:modes]
    out_ref[1] = filtered[half : half + modes]
    partners(lambda to: part_copy(to, mine).wait_send())


def local(n_freq, n_bl, vis_time, owner, counts, factors):
    _, _, base_here, samples = vis_time.shape
    modes = owner.shape[0]
    capacity, _, _, ranks, _ = factors.shape
    half = -(-2 * modes // 128) * 64
    rows = capacity * 2 * ranks
    wide = min(n_freq, 8) * rows
    table = jnp.asarray(wave_table(modes, half, samples))
    stays = pl.BlockSpec(memory_space=pltpu.HBM)
    out = pl.pallas_call(
        functools.partial(kernel, (n_freq, n_bl, modes, half, capacity, ranks)),
        out_shape=pltpu.VMEM((2, modes, base_here), BF16),
        in_specs=[stays] * 5,
        out_specs=pl.BlockSpec(memory_space=pltpu.VMEM),
        scratch_shapes=[
            pltpu.VMEM((CHUNKS, 2, base_here, samples // CHUNKS), BF16),
            pltpu.VMEM((samples, 2 * half), BF16),
            pltpu.VMEM((1, modes), jnp.int32),
            pltpu.VMEM((n_freq, modes), jnp.int32),
            pltpu.VMEM((n_freq, capacity, 2, ranks, base_here), BF16),
            pltpu.VMEM((n_freq * rows, base_here), BF16),
            pltpu.VMEM((n_freq * rows // wide, 2 * half, wide), BF16),
            pltpu.VMEM((8, 2 * half), F32),
            pltpu.VMEM((8, 2 * half), F32),
            pltpu.VMEM((base_here, 2 * half), BF16),
            pltpu.VMEM((n_bl, 2 * ranks, 2 * half), F32),
            pltpu.SemaphoreType.DMA((CHUNKS,)),
            pltpu.SemaphoreType.DMA((CHUNKS,)),
            pltpu.SemaphoreType.DMA((3,)),
            pltpu.SemaphoreType.DMA((n_freq,)),
            pltpu.SemaphoreType.DMA((n_freq,)),
            pltpu.SemaphoreType.DMA((n_bl,)),
            pltpu.SemaphoreType.DMA((n_bl,)),
        ],
        compiler_params=pltpu.CompilerParams(
            collective_id=0, has_side_effects=True, vmem_limit_bytes=63 * 1024 * 1024
        ),
    )(vis_time, table, owner.T, counts.T, factors)
    return out.transpose(0, 2, 1)[None]


def solution(mesh):
    placed = (P("freq", None, "bl", None), P(), P(), P("freq", None, None, None, "bl"))
    return jax.shard_map(
        functools.partial(local, mesh.shape["freq"], mesh.shape["bl"]),
        mesh=mesh, in_specs=placed, out_specs=P("freq", None, "bl", None), check_vma=False,
    )
```
